32 devices in a mesh: groups: 2 (over y), span: 8 (over z, x), sub: 2 (over core).
Axes of the slice: x: 2, y: 2, z: 4, core: 2. Of those that a mesh axis runs over, the one named last changes fastest.
Arguments:
- child_weight: float32 [4096, 128], P(('groups', 'span', 'sub')), parts along dimension 0, may hold values from 0.02 to 1
- child_mean: float32 [3, 4096, 128], P(None, ('groups', 'span', 'sub')), parts along dimension 1, may hold values from -6 to 6
- child_factor: float32 [6, 4096, 128], P(None, ('groups', 'span', 'sub')), parts along dimension 1, may hold values from 0.2 to 1
- child_colour: bfloat16 [48, 4096, 128], P(None, ('groups', 'span', 'sub')), parts along dimension 1, may hold values from -6 to 6
- child_dest: int32 [4096], P(('groups', 'span', 'sub')), parts along dimension 0, may hold values from 0 to 7, as said below
- child_slot: int32 [4096], P(('groups', 'span', 'sub')), parts along dimension 0, may hold values from 0 to 63
- child_row: int32 [4096, 128], P(('groups', 'span', 'sub')), parts along dimension 0, may hold values from 0 to 127
- live_blocks: int32 [32], P(('groups', 'span', 'sub')), parts along dimension 0, may hold values from 96 to 128, as said below
- parent_owner: int32 [1024], P(('groups', 'span', 'sub')), parts along dimension 0, may hold values from 0 to 7, as said below
- parent_slot: int32 [1024], P(('groups', 'span', 'sub')), parts along dimension 0, may hold values from 0 to 15
- parent_row: int32 [1024, 128], P(('groups', 'span', 'sub')), parts along dimension 0, may hold values from 0 to 127
Outputs:
- level_one: float32 [58, 1024, 128], P(None, ('groups', 'span', 'sub')), parts along dimension 1
- level_two: float32 [58, 256, 128], P(None, ('groups', 'span', 'sub')), parts along dimension 1
The draws below stay inside these ranges and needn't reach their ends.
There are 2 independent parts, one for each index of `groups`. The reference program is written for one: setup_inputs(seed, part) draws one part's arguments, and reference() takes and returns one part's arrays. A program takes and returns all parts, laid end to end along the dimension named above; each array names one. Nothing has to cross between parts.
Inputs may be any that keep to these rules, and one draw needn't show every extreme that they name: `child_dest`: among the live blocks of one device at most 32 name the same owner span. `live_blocks`: the live child blocks of a device are its first ones; the others are ignored. `parent_owner`: among the level-one blocks of one device at most 4 name the same owner span.
All inputs are finite; a program needn't handle non-finite values.
Results may differ from the reference program's by a relative error of at most 0.0003.
Values sent between devices are 32-bit elements; how exact they have to be, the bound alone decides.
No kernel may reach another device: no remote copies, remote signals or barrier semaphores. Data moves between devices by JAX's collectives and lax.ppermute only.
A program may use at most 64 MiB of HBM per device.

```python
import math
import jax
import jax.numpy as jnp
from jax import lax

ROWS = 128
COLOUR = 48
BLK = 128
PB_DEV = 32
CAP1 = 32
CAP2 = 4
PB_SPAN = 64
GB_SPAN = 16
CBLOCKS = 2048
PBLOCKS = 512
N_SPAN = 8
N_SUB = 2


def choose_owners(key, slots_each, taken, favoured, devices):
    rank_key, device_key = jax.random.split(key)
    ranking = jax.random.permutation(rank_key, N_SPAN)
    popular = (ranking < favoured).astype(jnp.int32)
    slot_total = N_SPAN * slots_each
    owner_of = jnp.arange(slot_total, dtype=jnp.int32) // slots_each

    def one_device(subkey):
        noise = jax.random.randint(subkey, (slot_total,), 0, 65536, dtype=jnp.int32)
        score = (popular[owner_of] * 65536 + noise) * slot_total + jnp.arange(slot_total, dtype=jnp.int32)
        return lax.top_k(score, taken)[1] // slots_each
    picked = jax.vmap(one_device)(jax.random.split(device_key, devices))
    return picked.reshape(-1).astype(jnp.int32)


def draw_child_dest(key, part):
    key = jax.random.fold_in(key, 11)
    return choose_owners(key, CAP1, BLK, max(1, N_SPAN // 4), N_SPAN * N_SUB)


def draw_parent_owner(key, part):
    key = jax.random.fold_in(key, 23)
    return choose_owners(key, CAP2, PB_DEV, max(1, N_SPAN // 8), N_SPAN * N_SUB)


def draw_live_blocks(key, part):
    key = jax.random.fold_in(key, 37)
    value_key, pick_key = jax.random.split(key)
    devices = N_SPAN * N_SUB
    values = jax.random.randint(value_key, (devices,), BLK - BLK // 4, BLK + 1, dtype=jnp.int32)
    chosen = jax.random.randint(pick_key, (), 0, devices, dtype=jnp.int32)
    return jnp.where(jnp.arange(devices, dtype=jnp.int32) == chosen, BLK, values).astype(jnp.int32)


def plant(drawn, key, least, largest):
    extent = drawn.shape
    index_at = [jax.random.randint(jax.random.fold_in(key, axis), (), 0, extent[axis]) for axis in range(len(extent))]
    drawn = drawn.at[tuple(index_at)].set(least)
    longest = extent.index(max(extent))
    index_at[longest] = (index_at[longest] + 1) % extent[longest]
    return drawn.at[tuple(index_at)].set(largest)


def block_scale(stream_key, dims, shards, least, high):
    factor_of = 1.0
    for axis_at, blocks in shards:
        draws = jax.random.uniform(jax.random.fold_in(jax.random.fold_in(stream_key, 6), axis_at), (blocks,), jnp.float32, least / len(shards), high / len(shards))
        factor_of = factor_of * jnp.repeat(jnp.exp(draws), dims[axis_at] // blocks).reshape((-1,) + (1,) * (len(dims) - 1 - axis_at))
    return factor_of


def normal_values(rng, dims, scale, bound, cuts=(), held_as=jnp.bfloat16):
    factor_of = block_scale(rng, dims, cuts, -0.22, 0.18) if cuts else 1.0
    drawn = jax.random.normal(rng, dims, jnp.float32) * scale * factor_of
    return jnp.minimum(jnp.maximum(drawn, -bound), bound).astype(held_as)


def setup_inputs(seed: int = 0, part: int = 0) -> dict:
    arg_keys = jax.random.split(jax.random.key(seed), 12)
    part_keys = jax.random.split(jax.random.fold_in(arg_keys[11], part), 12)
    return {
        "child_weight": jnp.clip(jnp.exp(math.log(1.0) - 3.912023 * jax.random.uniform(part_keys[0], (CBLOCKS, ROWS), jnp.float32) ** block_scale(part_keys[0], (CBLOCKS, ROWS), ((0, 16),), -0.2, 0.2)), 0.02, 1.0),
        "child_mean": normal_values(part_keys[1], (3, CBLOCKS, ROWS), 1.0, 6.0, ((1, 16),), jnp.float32),
        "child_factor": jnp.clip(0.2 + 0.8 * jax.random.uniform(part_keys[2], (6, CBLOCKS, ROWS), jnp.float32) ** block_scale(part_keys[2], (6, CBLOCKS, ROWS), ((1, 16),), -0.2, 0.2), 0.2, 1.0),
        "child_colour": normal_values(part_keys[3], (COLOUR, CBLOCKS, ROWS), 1.0, 6.0, ((1, 16),)),
        "child_dest": draw_child_dest(jax.random.fold_in(jax.random.fold_in(arg_keys[11], part), 71), part),
        "child_slot": plant(jax.random.randint(part_keys[5], (CBLOCKS,), 0, PB_SPAN), jax.random.fold_in(part_keys[5], 1), 0, PB_SPAN - 1).astype(jnp.int32),
        "child_row": plant(jax.random.randint(part_keys[6], (CBLOCKS, ROWS), 0, ROWS), jax.random.fold_in(part_keys[6], 1), 0, ROWS - 1).astype(jnp.int32),
        "live_blocks": draw_live_blocks(jax.random.fold_in(jax.random.fold_in(arg_keys[11], part), 71), part),
        "parent_owner": draw_parent_owner(jax.random.fold_in(jax.random.fold_in(arg_keys[11], part), 71), part),
        "parent_slot": plant(jax.random.randint(part_keys[9], (PBLOCKS,), 0, GB_SPAN), jax.random.fold_in(part_keys[9], 1), 0, GB_SPAN - 1).astype(jnp.int32),
        "parent_row": plant(jax.random.randint(part_keys[10], (PBLOCKS, ROWS), 0, ROWS), jax.random.fold_in(part_keys[10], 1), 0, ROWS - 1).astype(jnp.int32),
    }


PAIRS = ((0, 0), (0, 1), (0, 2), (1, 1), (1, 2), (2, 2))
WEIGHT_FLOOR = 0.1


def covariance(factor):
    return jnp.stack([
        factor[0] * factor[0],
        factor[0] * factor[1],
        factor[0] * factor[3],
        factor[1] * factor[1] + factor[2] * factor[2],
        factor[1] * factor[3] + factor[2] * factor[4],
        factor[3] * factor[3] + factor[4] * factor[4] + factor[5] * factor[5],
    ])


def moment_sums(weight, centres, factor, colour):
    outer = jnp.stack([centres[first] * centres[second] for first, second in PAIRS])
    return jnp.concatenate([weight[None], weight * centres, weight * (covariance(factor) + outer),
                            weight * colour.astype(jnp.float32)], 0)


def match_moments(sums):
    whole_weight = sums[0]
    divisor = jnp.maximum(whole_weight, WEIGHT_FLOOR)
    centre = sums[1:4] / divisor
    centre_outer = jnp.stack([centre[first] * centre[second] for first, second in PAIRS])
    spread = sums[4:10] / divisor - centre_outer
    colour_mean = sums[10:] / divisor
    return jnp.concatenate([whole_weight[None], centre, spread, colour_mean], 0)


def reference(child_weight, child_mean, child_factor, child_colour, child_dest, child_slot, child_row,
              live_blocks, parent_owner, parent_slot, parent_row):
    components = 10 + COLOUR
    parent_cells = N_SPAN * PB_SPAN * ROWS

    def add_device(collected, device):
        start = device * BLK
        weight = lax.dynamic_slice_in_dim(child_weight, start, BLK, 0)
        centres = lax.dynamic_slice_in_dim(child_mean, start, BLK, 1)
        factor = lax.dynamic_slice_in_dim(child_factor, start, BLK, 1)
        colour = lax.dynamic_slice_in_dim(child_colour, start, BLK, 1)
        owners = lax.dynamic_slice_in_dim(child_dest, start, BLK, 0)
        slots = lax.dynamic_slice_in_dim(child_slot, start, BLK, 0)
        rows_of = lax.dynamic_slice_in_dim(child_row, start, BLK, 0)
        live_count = lax.dynamic_index_in_dim(live_blocks, device, 0, keepdims=False)
        moments = moment_sums(weight, centres, factor, colour)
        targets = (owners * PB_SPAN + slots)[:, None] * ROWS + rows_of
        is_live = jnp.arange(BLK, dtype=jnp.int32) < live_count
        targets = jnp.where(is_live[:, None], targets, parent_cells).astype(jnp.int32)
        collected = collected.at[:, targets.reshape(-1)].add(moments.reshape(components, -1), mode="drop")
        return collected, None

    start_sums = jnp.zeros((components, parent_cells), jnp.float32)
    sums_one = lax.scan(add_device, start_sums, jnp.arange(N_SPAN * N_SUB, dtype=jnp.int32))[0]
    level_one = match_moments(sums_one).reshape(components, N_SPAN * PB_SPAN, ROWS)
    targets_two = ((parent_owner * GB_SPAN + parent_slot)[:, None] * ROWS + parent_row).astype(jnp.int32)
    sums_two = jnp.zeros((components, N_SPAN * GB_SPAN * ROWS), jnp.float32)
    sums_two = sums_two.at[:, targets_two.reshape(-1)].add(sums_one)
    level_two = match_moments(sums_two).reshape(components, N_SPAN * GB_SPAN, ROWS)
    return level_one, level_two
```

```python
import math

import jax
import jax.numpy as jnp
from jax import lax
from jax.experimental import pallas as pl
from jax.experimental.pallas import tpu as pltpu
from jax.sharding import PartitionSpec as P

PB_DEV = 32
GB_DEV = 8


PAIRS = ((0, 0), (0, 1), (0, 2), (1, 1), (1, 2), (2, 2))
WEIGHT_FLOOR = 0.1


def covariance(factor):
    return jnp.stack(
        [
            factor[0] * factor[0],
            factor[0] * factor[1],
            factor[0] * factor[3],
            factor[1] * factor[1] + factor[2] * factor[2],
            factor[1] * factor[3] + factor[2] * factor[4],
            factor[3] * factor[3] + factor[4] * factor[4] + factor[5] * factor[5],
        ]
    )


def moment_sums(weight, centres, factor, colour):
    outer = jnp.stack([centres[first] * centres[second] for first, second in PAIRS])
    return jnp.concatenate(
        [
            weight[None],
            weight * centres,
            weight * (covariance(factor) + outer),
            weight * colour.astype(jnp.float32),
        ],
        0,
    )


def match_moments(sums):
    whole_weight = sums[0]
    divisor = jnp.maximum(whole_weight, WEIGHT_FLOOR)
    centre = sums[1:4] / divisor
    centre_outer = jnp.stack([centre[first] * centre[second] for first, second in PAIRS])
    spread = sums[4:10] / divisor - centre_outer
    colour_mean = sums[10:] / divisor
    return jnp.concatenate([whole_weight[None], centre, spread, colour_mean], 0)


def earlier_same(owners):
    position = jnp.arange(owners.shape[0], dtype=jnp.int32)
    same_owner = (owners[:, None] == owners[None, :]) & (position[None, :] < position[:, None])
    return jnp.sum(same_owner.astype(jnp.int32), 1)


def fold_rows(values, row_picks):
    block_total = values.shape[1]
    width = values.shape[2]
    group_size = math.gcd(block_total, 16)
    row_labels = jnp.arange(width, dtype=jnp.int32)

    def fold_step(turn_index, result):
        start = turn_index * group_size
        block_part = lax.dynamic_slice_in_dim(values, start, group_size, 1)
        picks_part = lax.dynamic_slice_in_dim(row_picks, start, group_size, 0)
        row_table = (picks_part[:, :, None] == row_labels).astype(jnp.float32)
        folded_part = jnp.einsum(
            "cbr,brj->cbj", block_part, row_table, precision=lax.Precision.HIGHEST
        )
        return lax.dynamic_update_slice_in_dim(result, folded_part, start, 1)

    return lax.fori_loop(
        0, block_total // group_size, fold_step, jnp.zeros(values.shape, jnp.float32)
    )


def place_blocks(values, block_picks, block_count):
    block_table = (block_picks[:, None] == jnp.arange(block_count, dtype=jnp.int32)).astype(
        jnp.float32
    )
    return jnp.einsum("csj,sp->cpj", values, block_table, precision=lax.Precision.HIGHEST)


def seam(partial_value, per_device):
    whole_sum = lax.psum(partial_value, "sub")
    return lax.dynamic_slice_in_dim(whole_sum, lax.axis_index("sub") * per_device, per_device, 1)


def plain_body(
    child_weight,
    child_mean,
    child_factor,
    child_colour,
    child_dest,
    child_slot,
    child_row,
    live_blocks,
    parent_owner,
    parent_slot,
    parent_row,
):
    spans = lax.axis_size("span")
    sub_count = lax.axis_size("sub")
    block_count = child_weight.shape[0]
    row_count = child_weight.shape[1]
    components = 10 + child_colour.shape[0]
    cap_one = max(2, (2 * block_count + spans - 1) // spans)
    slot_total = spans * cap_one
    parent_span = PB_DEV * sub_count
    moments = moment_sums(child_weight, child_mean, child_factor, child_colour)
    position = jnp.arange(block_count, dtype=jnp.int32)
    is_live = position < live_blocks[0]
    slot_index = jnp.where(is_live, child_dest * cap_one + earlier_same(child_dest), slot_total)
    outgoing_shape = (components, slot_total, row_count)
    outgoing = jnp.zeros(outgoing_shape, jnp.float32).at[:, slot_index].set(moments, mode="drop")
    targets = child_slot[:, None] * row_count + child_row
    target_rows = (
        jnp.zeros((1, slot_total, row_count), jnp.int32).at[0, slot_index].set(targets, mode="drop")
    )
    received, received_rows = (
        lax.all_to_all(outgoing, "span", split_axis=1, concat_axis=1, tiled=True),
        lax.all_to_all(target_rows, "span", split_axis=1, concat_axis=1, tiled=True),
    )
    incoming_rows = received_rows[0]
    folded = fold_rows(received, incoming_rows % row_count)
    collected = place_blocks(folded, incoming_rows[:, 0] // row_count, parent_span)
    own_sums = seam(collected, PB_DEV)
    level_one = match_moments(own_sums)
    cap_two = max(1, (PB_DEV + spans - 1) // spans)
    slot_two = parent_owner * cap_two + earlier_same(parent_owner)
    outgoing_two = (
        jnp.zeros((components, spans * cap_two, row_count), jnp.float32)
        .at[:, slot_two]
        .set(own_sums)
    )
    targets_two = parent_slot[:, None] * row_count + parent_row
    rows_two = (
        jnp.zeros((1, spans * cap_two, row_count), jnp.int32).at[0, slot_two].set(targets_two)
    )
    received_two, received_rows_two = (
        lax.all_to_all(outgoing_two, "span", split_axis=1, concat_axis=1, tiled=True),
        lax.all_to_all(rows_two, "span", split_axis=1, concat_axis=1, tiled=True),
    )
    grand_span = GB_DEV * sub_count
    incoming_two = received_rows_two[0]
    folded_two = fold_rows(received_two, incoming_two % row_count)
    collected_two = place_blocks(folded_two, incoming_two[:, 0] // row_count, grand_span)
    level_two = match_moments(seam(collected_two, GB_DEV))
    return (level_one, level_two)


TILE = 8
UNROLL = 8


def tile_count(width, slots):
    return (width // TILE) * slots + (slots * (width % TILE) + TILE - 1) // TILE


def split_pair(values):
    high = values.astype(jnp.bfloat16)
    low = (values - high.astype(jnp.float32)).astype(jnp.bfloat16)
    return jnp.concatenate([high, low], 1)


def row_table(rows):
    width = rows.shape[1]
    labels = lax.broadcasted_iota(jnp.int32, (width, width), 0)
    picks = jnp.where(labels == rows, 1.0, 0.0).astype(jnp.bfloat16)
    return jnp.concatenate([picks, picks], 1)


def fold_block(values, rows):
    return lax.dot_general(
        split_pair(values),
        row_table(rows),
        (((1,), (1,)), ((), ())),
        preferred_element_type=jnp.float32,
    )


def group_mask(extra, group):
    return lax.broadcasted_iota(jnp.int32, (TILE, 1), 0) // extra == group


def child_kernel(first, width, regions, slots, *refs):
    geometry = first == 0
    (pos_ref, live_ref, rows_ref, weight_ref, mean_ref, factor_ref, colour_ref) = refs[:7]
    keep_ref, send_ref = refs[7:9]
    moments, totals, colours, load_sem, keep_sem, send_sem = refs[9:]
    block_count, row_count = rows_ref.shape
    full, extra = width // TILE, width % TILE
    per_region = tile_count(width, slots)
    group = 16
    first_colour = max(first, 10) - 10
    colour_total = colours.shape[0]
    load = None
    if first + width > 10:
        load = pltpu.make_async_copy(
            colour_ref.at[pl.ds(first_colour, colour_total)], colours, load_sem
        )
        load.start()

    def clear(step, carry):
        totals[pl.ds(step * 16, 16)] = jnp.zeros((16, TILE, row_count), jnp.float32)
        return carry

    lax.fori_loop(0, totals.shape[0] // 16, clear, 0)
    if load is not None:
        load.wait()

    def prepare(step, carry):
        start = pl.multiple_of(step * group, group)
        part = pl.ds(start, group)
        weight = weight_ref[part, :]
        values = {}
        if geometry:
            centre = [mean_ref[axis, part, :] for axis in range(3)]
            factor = [factor_ref[entry, part, :] for entry in range(6)]
            spread = [
                factor[0] * factor[0],
                factor[0] * factor[1],
                factor[0] * factor[3],
                factor[1] * factor[1] + factor[2] * factor[2],
                factor[1] * factor[3] + factor[2] * factor[4],
                factor[3] * factor[3] + factor[4] * factor[4] + factor[5] * factor[5],
            ]
            values[0] = weight
            for axis in range(3):
                values[1 + axis] = weight * centre[axis]
            for entry, (left, right) in enumerate(PAIRS):
                values[4 + entry] = weight * (spread[entry] + centre[left] * centre[right])
        for entry in range(colour_total):
            values[10 + first_colour + entry] = weight * colours[entry, part, :].astype(jnp.float32)
        for place in range(full * TILE + (TILE if extra else 0)):
            component = first + (place if place < full * TILE else full * TILE + place % extra)
            moments[pl.ds(place * block_count + start, group), :] = values[component]
        return carry

    lax.fori_loop(0, block_count // group, prepare, 0)
    live = live_ref[0]

    def fold(step, carry):
        folded = []
        for turn in range(UNROLL):
            block = step * UNROLL + turn
            place = pos_ref[block]
            region, slot = place // slots, place % slots
            lines = [
                moments[pl.ds(tile * TILE * block_count + block, TILE, stride=block_count), :]
                for tile in range(full)
            ]
            if extra:
                line = moments[pl.ds(full * TILE * block_count + block, TILE, stride=block_count), :]
                lines.append(jnp.where(group_mask(extra, slot % (TILE // extra)), line, 0.0))
            rows = jnp.where(block < live, rows_ref[pl.ds(block, 1), :], -1)
            folded.append((region * per_region, slot, fold_block(jnp.concatenate(lines, 0), rows)))
        for base, slot, result in folded:
            for tile in range(full):
                totals[base + tile * slots + slot] += result[tile * TILE : (tile + 1) * TILE]
            if extra:
                totals[base + full * slots + slot // (TILE // extra)] += result[full * TILE :]
        return carry

    lax.fori_loop(0, (live + UNROLL - 1) // UNROLL, fold, 0)
    half = regions * per_region
    keep = pltpu.make_async_copy(totals.at[pl.ds(0, half)], keep_ref, keep_sem)
    send = pltpu.make_async_copy(totals.at[pl.ds(half, half)], send_ref, send_sem)
    send.start()
    keep.start()
    send.wait()
    keep.wait()


def fold_children(place, live, rows, weight, mean, factor, colour, first, width, regions, slots):
    block_count, row_count = rows.shape
    per_region = tile_count(width, slots)
    colour_total = max(first + width - max(first, 10), 0)
    padded = width // TILE * TILE + (TILE if width % TILE else 0)
    half = jax.ShapeDtypeStruct((regions * per_region, TILE, row_count), jnp.float32)
    whole = pl.BlockSpec(memory_space=pltpu.VMEM)
    scalars = pl.BlockSpec(memory_space=pltpu.SMEM)
    outside = pl.BlockSpec(memory_space=pl.ANY)

    def kernel(*refs):
        child_kernel(first, width, regions, slots, *refs)

    return pl.pallas_call(
        kernel,
        out_shape=(half, half),
        in_specs=[scalars, scalars, whole, whole, whole if first == 0 else outside]
        + [whole if first == 0 else outside, outside],
        out_specs=(outside, outside),
        scratch_shapes=[
            pltpu.VMEM((padded * block_count, row_count), jnp.float32),
            pltpu.VMEM((2 * regions * per_region, TILE, row_count), jnp.float32),
            pltpu.VMEM((max(colour_total, 1), block_count, row_count), jnp.bfloat16),
            pltpu.SemaphoreType.DMA,
            pltpu.SemaphoreType.DMA,
            pltpu.SemaphoreType.DMA,
        ],
        compiler_params=pltpu.CompilerParams(vmem_limit_bytes=48 * 1024 * 1024),
        cost_estimate=pl.CostEstimate(
            flops=4 * block_count * padded * row_count * row_count,
            bytes_accessed=16 * regions * per_region * TILE * row_count,
            transcendentals=0,
        ),
        name="fold_children",
    )(place, live, rows, weight, mean, factor, colour)


def parent_kernel(width, regions, cap, *refs):
    place_ref, rows_ref, sums_ref = refs[:3]
    out_refs, totals = refs[3:-1], refs[-1]
    block_count = rows_ref.shape[0]
    full, extra = width // TILE, width % TILE
    per_region = tile_count(width, cap)
    totals[...] = jnp.zeros(totals.shape, jnp.float32)
    for start in range(0, block_count, UNROLL):
        folded = []
        for block in range(start, start + UNROLL):
            place = place_ref[block]
            region, rank = place // cap, place % cap
            lines = [sums_ref[tile * block_count + block] for tile in range(full)]
            if extra:
                share = TILE // extra
                line = sums_ref[full * block_count + block // share]
                line = jnp.where(group_mask(extra, block % share), line, 0.0)
                line = sum(
                    (pltpu.roll(line, turn * extra, 0) for turn in range(1, share)), start=line
                )
                lines.append(jnp.where(group_mask(extra, rank % share), line, 0.0))
            rows = rows_ref[pl.ds(block, 1), :]
            folded.append((region * per_region, rank, fold_block(jnp.concatenate(lines, 0), rows)))
        for base, rank, result in folded:
            for tile in range(full):
                totals[base + tile * cap + rank] += result[tile * TILE : (tile + 1) * TILE]
            if extra:
                totals[base + full * cap + rank // (TILE // extra)] += result[full * TILE :]
    for region, out_ref in enumerate(out_refs):
        out_ref[...] = totals[region * per_region : (region + 1) * per_region]


def fold_parents(place, rows, sums, width, regions, cap):
    row_count = rows.shape[1]
    per_region = tile_count(width, cap)
    whole = pl.BlockSpec(memory_space=pltpu.VMEM)

    def kernel(*refs):
        parent_kernel(width, regions, cap, *refs)

    return pl.pallas_call(
        kernel,
        out_shape=[jax.ShapeDtypeStruct((per_region, TILE, row_count), jnp.float32)] * regions,
        in_specs=[pl.BlockSpec(memory_space=pltpu.SMEM), whole, whole],
        out_specs=[whole] * regions,
        scratch_shapes=[pltpu.VMEM((regions * per_region, TILE, row_count), jnp.float32)],
        compiler_params=pltpu.CompilerParams(vmem_limit_bytes=24 * 1024 * 1024),
        cost_estimate=pl.CostEstimate(
            flops=4 * rows.shape[0] * width * row_count * row_count,
            bytes_accessed=8 * regions * per_region * TILE * row_count,
            transcendentals=0,
        ),
        name="fold_parents",
    )(place, rows, sums)


def place_kernel(width, regions, cap, slots, *refs):
    code_ref, in_refs = refs[0], refs[1 : 1 + regions]
    keep_ref, send_ref, totals = refs[1 + regions :]
    full, extra = width // TILE, width % TILE
    per_half = tile_count(width, slots)
    totals[...] = jnp.zeros(totals.shape, jnp.float32)
    for region, in_ref in enumerate(in_refs):
        for rank in range(cap):
            code = code_ref[region * cap + rank]
            half, slot = code // slots, code % slots
            for tile in range(full):
                totals[half * per_half + tile * slots + slot] += in_ref[tile * cap + rank]
            if extra:
                share = TILE // extra
                line = in_ref[full * cap + rank // share]
                line = jnp.where(group_mask(extra, rank % share), line, 0.0)
                line = sum(
                    (pltpu.roll(line, turn * extra, 0) for turn in range(1, share)), start=line
                )
                line = jnp.where(group_mask(extra, slot % share), line, 0.0)
                totals[half * per_half + full * slots + slot // share] += line
    keep_ref[...] = totals[:per_half]
    send_ref[...] = totals[per_half:]


def place_parents(codes, parts, width, cap, slots):
    row_count = parts[0].shape[2]
    per_half = tile_count(width, slots)
    whole = pl.BlockSpec(memory_space=pltpu.VMEM)
    half = jax.ShapeDtypeStruct((per_half, TILE, row_count), jnp.float32)

    def kernel(*refs):
        place_kernel(width, len(parts), cap, slots, *refs)

    return pl.pallas_call(
        kernel,
        out_shape=(half, half),
        in_specs=[pl.BlockSpec(memory_space=pltpu.SMEM)] + [whole] * len(parts),
        out_specs=(whole, whole),
        scratch_shapes=[pltpu.VMEM((2 * per_half, TILE, row_count), jnp.float32)],
        compiler_params=pltpu.CompilerParams(vmem_limit_bytes=24 * 1024 * 1024),
        cost_estimate=pl.CostEstimate(
            flops=per_half * TILE * row_count,
            bytes_accessed=16 * per_half * TILE * row_count,
            transcendentals=0,
        ),
        name="place_parents",
    )(codes, *parts)


def unpack(tiles, width, slots):
    full, extra = width // TILE, width % TILE
    row_count = tiles.shape[2]
    whole = tiles[: full * slots].reshape(full, slots, TILE, row_count)
    whole = whole.transpose(0, 2, 1, 3).reshape(full * TILE, slots, row_count)
    if not extra:
        return whole
    rest = tiles[full * slots :].reshape(slots, extra, row_count).transpose(1, 0, 2)
    return jnp.concatenate([whole, rest], 0)


def merged_parts(parts):
    sums = parts[0]
    divisor = jnp.maximum(sums[0], WEIGHT_FLOOR)
    centre = sums[1:4] / divisor
    centre_outer = jnp.stack([centre[first] * centre[second] for first, second in PAIRS])
    spread = sums[4:10] / divisor - centre_outer
    rest = [part / divisor for part in [sums[10:]] + parts[1:] if part.shape[0]]
    return jnp.concatenate([sums[:1], centre, spread] + rest, 0)


def cut_components(components):
    chunks = [(0, 10, True)]
    start = 10
    while start < components:
        width = min(16, components - start)
        chunks.append((start, width, True))
        start += width
    return chunks


def span_body(
    child_weight,
    child_mean,
    child_factor,
    child_colour,
    child_dest,
    child_slot,
    child_row,
    live_blocks,
    parent_owner,
    parent_slot,
    parent_row,
):
    spans = lax.axis_size("span")
    columns = 2
    lines = spans // columns
    components = 10 + child_colour.shape[0]
    span_at, sub_at = lax.axis_index("span"), lax.axis_index("sub")
    cap_two = max(1, (PB_DEV + spans - 1) // spans)

    def region_of(owner):
        column = (owner % columns - span_at % columns) % columns
        line = (owner // columns - span_at // columns) % lines
        return column * lines + line

    def code_of(slot, per_device):
        return (slot // per_device - sub_at) % 2 * per_device + slot % per_device

    def shift(values, column, line):
        pairs = [
            (at, (at // columns + line) % lines * columns + (at + column) % columns)
            for at in range(spans)
        ]
        return lax.ppermute(values, "span", pairs)

    def swap(values):
        return lax.ppermute(values, "sub", [(0, 1), (1, 0)])

    code_one = code_of(child_slot, PB_DEV)
    place_one = (code_one // PB_DEV * spans + region_of(child_dest)) * PB_DEV + code_one % PB_DEV
    place_two = region_of(parent_owner) * cap_two + earlier_same(parent_owner)
    taken = place_two[None, :] == jnp.arange(spans * cap_two, dtype=jnp.int32)[:, None]
    codes = jnp.sum(jnp.where(taken, code_of(parent_slot, GB_DEV)[None, :], 0), 1)
    codes = codes.reshape(spans, cap_two)
    codes = jnp.concatenate(
        [codes[:1]]
        + [
            shift(codes[region : region + 1], region // lines, region % lines)
            for region in range(1, spans)
        ],
        0,
    ).reshape(-1)

    level_one, level_two = [], []
    for first, width, column_first in cut_components(components):
        keep, send = fold_children(
            place_one,
            live_blocks,
            child_row,
            child_weight,
            child_mean,
            child_factor,
            child_colour,
            first,
            width,
            spans,
            PB_DEV,
        )
        size = tile_count(width, PB_DEV)
        other = swap(send)
        if column_first:
            across = shift(keep[lines * size :] + other[lines * size :], 1, 0)

            def term(line):
                part = slice(line * size, (line + 1) * size)
                return keep[part] + other[part] + across[part]

            total = term(lines - 1)
            for line in range(lines - 2, -1, -1):
                total = shift(total, 0, 1) + term(line)
        else:
            both = (keep + other).reshape((columns, lines, size) + keep.shape[1:])
            total = both[:, lines - 1]
            for line in range(lines - 2, -1, -1):
                total = shift(total, 0, 1) + both[:, line]
            total = total[0] + shift(total[1], 1, 0)
        level_one.append(unpack(total, width, PB_DEV))
        parts = fold_parents(place_two, parent_row, total, width, spans, cap_two)
        parts = [parts[0]] + [
            shift(parts[region], region // lines, region % lines) for region in range(1, spans)
        ]
        keep_two, send_two = place_parents(codes, parts, width, cap_two, GB_DEV)
        level_two.append(unpack(keep_two + swap(send_two), width, GB_DEV))
    return (merged_parts(level_one), merged_parts(level_two))


def body(*arrays):
    spans, subs = lax.axis_size("span"), lax.axis_size("sub")
    blocks = arrays[0].shape[0]
    dense = spans * subs * PB_DEV
    fits = subs == 2 and spans % 2 == 0 and dense <= 4 * blocks and PB_DEV % (4 * spans) == 0
    if fits and blocks % 16 == 0:
        return span_body(*arrays)
    return plain_body(*arrays)


def solution(mesh):
    placed = (
        P(("groups", "span", "sub"), None),
        P(None, ("groups", "span", "sub"), None),
        P(None, ("groups", "span", "sub"), None),
        P(None, ("groups", "span", "sub"), None),
        P(("groups", "span", "sub")),
        P(("groups", "span", "sub")),
        P(("groups", "span", "sub"), None),
        P(("groups", "span", "sub")),
        P(("groups", "span", "sub")),
        P(("groups", "span", "sub")),
        P(("groups", "span", "sub"), None),
    )
    return jax.shard_map(
        body,
        mesh=mesh,
        in_specs=placed,
        out_specs=(
            P(None, ("groups", "span", "sub"), None),
            P(None, ("groups", "span", "sub"), None),
        ),
        check_vma=False,
    )
```

```python
import math

import jax
import jax.numpy as jnp
from jax import lax
from jax.experimental import pallas as pl
from jax.experimental.pallas import tpu as pltpu
from jax.sharding import PartitionSpec as P

PB_DEV = 32
GB_DEV = 8


PAIRS = ((0, 0), (0, 1), (0, 2), (1, 1), (1, 2), (2, 2))
WEIGHT_FLOOR = 0.1


def covariance(factor):
    return jnp.stack(
        [
            factor[0] * factor[0],
            factor[0] * factor[1],
            factor[0] * factor[3],
            factor[1] * factor[1] + factor[2] * factor[2],
            factor[1] * factor[3] + factor[2] * factor[4],
            factor[3] * factor[3] + factor[4] * factor[4] + factor[5] * factor[5],
        ]
    )


def moment_sums(weight, centres, factor, colour):
    outer = jnp.stack([centres[first] * centres[second] for first, second in PAIRS])
    return jnp.concatenate(
        [
            weight[None],
            weight * centres,
            weight * (covariance(factor) + outer),
            weight * colour.astype(jnp.float32),
        ],
        0,
    )


def match_moments(sums):
    whole_weight = sums[0]
    divisor = jnp.maximum(whole_weight, WEIGHT_FLOOR)
    centre = sums[1:4] / divisor
    centre_outer = jnp.stack([centre[first] * centre[second] for first, second in PAIRS])
    spread = sums[4:10] / divisor - centre_outer
    colour_mean = sums[10:] / divisor
    return jnp.concatenate([whole_weight[None], centre, spread, colour_mean], 0)


def earlier_same(owners):
    position = jnp.arange(owners.shape[0], dtype=jnp.int32)
    same_owner = (owners[:, None] == owners[None, :]) & (position[None, :] < position[:, None])
    return jnp.sum(same_owner.astype(jnp.int32), 1)


def fold_rows(values, row_picks):
    block_total = values.shape[1]
    width = values.shape[2]
    group_size = math.gcd(block_total, 16)
    row_labels = jnp.arange(width, dtype=jnp.int32)

    def fold_step(turn_index, result):
        start = turn_index * group_size
        block_part = lax.dynamic_slice_in_dim(values, start, group_size, 1)
        picks_part = lax.dynamic_slice_in_dim(row_picks, start, group_size, 0)
        row_table = (picks_part[:, :, None] == row_labels).astype(jnp.float32)
        folded_part = jnp.einsum(
            "cbr,brj->cbj", block_part, row_table, precision=lax.Precision.HIGHEST
        )
        return lax.dynamic_update_slice_in_dim(result, folded_part, start, 1)

    return lax.fori_loop(
        0, block_total // group_size, fold_step, jnp.zeros(values.shape, jnp.float32)
    )


def place_blocks(values, block_picks, block_count):
    block_table = (block_picks[:, None] == jnp.arange(block_count, dtype=jnp.int32)).astype(
        jnp.float32
    )
    return jnp.einsum("csj,sp->cpj", values, block_table, precision=lax.Precision.HIGHEST)


def seam(partial_value, per_device):
    whole_sum = lax.psum(partial_value, "sub")
    return lax.dynamic_slice_in_dim(whole_sum, lax.axis_index("sub") * per_device, per_device, 1)


def plain_body(
    child_weight,
    child_mean,
    child_factor,
    child_colour,
    child_dest,
    child_slot,
    child_row,
    live_blocks,
    parent_owner,
    parent_slot,
    parent_row,
):
    spans = lax.axis_size("span")
    sub_count = lax.axis_size("sub")
    block_count = child_weight.shape[0]
    row_count = child_weight.shape[1]
    components = 10 + child_colour.shape[0]
    cap_one = max(2, (2 * block_count + spans - 1) // spans)
    slot_total = spans * cap_one
    parent_span = PB_DEV * sub_count
    moments = moment_sums(child_weight, child_mean, child_factor, child_colour)
    position = jnp.arange(block_count, dtype=jnp.int32)
    is_live = position < live_blocks[0]
    slot_index = jnp.where(is_live, child_dest * cap_one + earlier_same(child_dest), slot_total)
    outgoing_shape = (components, slot_total, row_count)
    outgoing = jnp.zeros(outgoing_shape, jnp.float32).at[:, slot_index].set(moments, mode="drop")
    targets = child_slot[:, None] * row_count + child_row
    target_rows = (
        jnp.zeros((1, slot_total, row_count), jnp.int32).at[0, slot_index].set(targets, mode="drop")
    )
    received, received_rows = (
        lax.all_to_all(outgoing, "span", split_axis=1, concat_axis=1, tiled=True),
        lax.all_to_all(target_rows, "span", split_axis=1, concat_axis=1, tiled=True),
    )
    incoming_rows = received_rows[0]
    folded = fold_rows(received, incoming_rows % row_count)
    collected = place_blocks(folded, incoming_rows[:, 0] // row_count, parent_span)
    own_sums = seam(collected, PB_DEV)
    level_one = match_moments(own_sums)
    cap_two = max(1, (PB_DEV + spans - 1) // spans)
    slot_two = parent_owner * cap_two + earlier_same(parent_owner)
    outgoing_two = (
        jnp.zeros((components, spans * cap_two, row_count), jnp.float32)
        .at[:, slot_two]
        .set(own_sums)
    )
    targets_two = parent_slot[:, None] * row_count + parent_row
    rows_two = (
        jnp.zeros((1, spans * cap_two, row_count), jnp.int32).at[0, slot_two].set(targets_two)
    )
    received_two, received_rows_two = (
        lax.all_to_all(outgoing_two, "span", split_axis=1, concat_axis=1, tiled=True),
        lax.all_to_all(rows_two, "span", split_axis=1, concat_axis=1, tiled=True),
    )
    grand_span = GB_DEV * sub_count
    incoming_two = received_rows_two[0]
    folded_two = fold_rows(received_two, incoming_two % row_count)
    collected_two = place_blocks(folded_two, incoming_two[:, 0] // row_count, grand_span)
    level_two = match_moments(seam(collected_two, GB_DEV))
    return (level_one, level_two)


TILE = 8
UNROLL = 8
WIDTHS = (16, 16, 8, 8)
GROUPS = {6: (0, 1, 2, 3, 4)}
WAIT_FETCH = True
HEAD = 1


def tile_count(width, slots):
    return (width // TILE) * slots + (slots * (width % TILE) + TILE - 1) // TILE


def split_pair(values):
    high = values.astype(jnp.bfloat16)
    low = (values - high.astype(jnp.float32)).astype(jnp.bfloat16)
    return jnp.concatenate([high, low], 1)


def row_table(rows):
    width = rows.shape[1]
    labels = lax.broadcasted_iota(jnp.int32, (width, width), 0)
    picks = jnp.where(labels == rows, 1.0, 0.0).astype(jnp.bfloat16)
    return jnp.concatenate([picks, picks], 1)


def fold_block(values, rows):
    return lax.dot_general(
        split_pair(values),
        row_table(rows),
        (((1,), (1,)), ((), ())),
        preferred_element_type=jnp.float32,
    )


def tile_rows():
    return lax.broadcasted_iota(jnp.int32, (TILE, 1), 0)


def spread_group(line, extra, group):
    share = TILE // extra
    line = jnp.where(tile_rows() // extra == group, line, 0.0)
    return sum((pltpu.roll(line, turn * extra, 0) for turn in range(1, share)), start=line)


def child_kernel(first, width, regions, slots, *refs):
    geometry = first == 0
    place_ref, live_ref = refs[:2]
    count = 4 if geometry else 3
    sources = refs[2 : 2 + count]
    keep_ref, send_ref = refs[2 + count : 4 + count]
    targets = refs[4 + count : 4 + 2 * count]
    rows_ref, weight_ref = targets[:2]
    moments, totals, load_sems, out_sems = refs[4 + 2 * count :]
    block_count, row_count = rows_ref.shape
    full, extra = width // TILE, width % TILE
    per_region = tile_count(width, slots)
    group = 16
    first_colour = max(first, 10) - 10
    colour_total = 0 if geometry else width
    loads = []
    for at, (source, target) in enumerate(zip(sources, targets, strict=True)):
        if colour_total and at == 2:
            source = source.at[pl.ds(first_colour, colour_total)]
        loads.append(pltpu.make_async_copy(source, target, load_sems.at[at]))
    if geometry:
        mean_ref, factor_ref = targets[2:4]
    else:
        colours = targets[2]
    for load in loads:
        load.start()

    def clear(step, carry):
        totals[pl.ds(step * 16, 16)] = jnp.zeros((16, TILE, row_count), jnp.float32)
        return carry

    lax.fori_loop(0, totals.shape[0] // 16, clear, 0)
    for load in loads:
        load.wait()

    def prepare(step, carry):
        start = pl.multiple_of(step * group, group)
        part = pl.ds(start, group)
        weight = weight_ref[part, :]
        values = {}
        if geometry:
            centre = [mean_ref[axis, part, :] for axis in range(3)]
            factor = [factor_ref[entry, part, :] for entry in range(6)]
            spread = [
                factor[0] * factor[0],
                factor[0] * factor[1],
                factor[0] * factor[3],
                factor[1] * factor[1] + factor[2] * factor[2],
                factor[1] * factor[3] + factor[2] * factor[4],
                factor[3] * factor[3] + factor[4] * factor[4] + factor[5] * factor[5],
            ]
            values[0] = weight
            for axis in range(3):
                values[1 + axis] = weight * centre[axis]
            for entry, (left, right) in enumerate(PAIRS):
                values[4 + entry] = weight * (spread[entry] + centre[left] * centre[right])
        for entry in range(colour_total):
            values[10 + first_colour + entry] = weight * colours[entry, part, :].astype(jnp.float32)
        for place in range(full * TILE + (TILE if extra else 0)):
            component = first + (place if place < full * TILE else full * TILE + place % extra)
            moments[pl.ds(place * block_count + start, group), :] = values[component]
        return carry

    lax.fori_loop(0, block_count // group, prepare, 0)
    live = live_ref[0]

    def fold(step, carry):
        folded = []
        for turn in range(UNROLL):
            block = step * UNROLL + turn
            place = place_ref[block]
            region, slot = place // slots, place % slots
            lines = [
                moments[pl.ds(tile * TILE * block_count + block, TILE, stride=block_count), :]
                for tile in range(full)
            ]
            if extra:
                line = moments[pl.ds(full * TILE * block_count + block, TILE, stride=block_count), :]
                lines.append(jnp.where(tile_rows() // extra == slot % (TILE // extra), line, 0.0))
            rows = jnp.where(block < live, rows_ref[pl.ds(block, 1), :], -1)
            folded.append((region * per_region, slot, fold_block(jnp.concatenate(lines, 0), rows)))
        for base, slot, result in folded:
            for tile in range(full):
                totals[base + tile * slots + slot] += result[tile * TILE : (tile + 1) * TILE]
            if extra:
                totals[base + full * slots + slot // (TILE // extra)] += result[full * TILE :]
        return carry

    lax.fori_loop(0, (live + UNROLL - 1) // UNROLL, fold, 0)
    half = regions * per_region
    send = pltpu.make_async_copy(totals.at[pl.ds(half, half)], send_ref, out_sems.at[0])
    keep = pltpu.make_async_copy(totals.at[pl.ds(0, half)], keep_ref, out_sems.at[1])
    send.start()
    keep.start()
    send.wait()
    keep.wait()


def fold_children(place, live, arrays, first, width, regions, slots, vmem):
    rows, weight, mean, factor, colour = arrays
    geometry = first == 0
    used = [rows, weight, mean, factor] if geometry else [rows, weight, colour]
    block_count, row_count = rows.shape
    per_region = tile_count(width, slots)
    padded = width // TILE * TILE + (TILE if width % TILE else 0)
    half = jax.ShapeDtypeStruct((regions * per_region, TILE, row_count), jnp.float32)
    scalars = pl.BlockSpec(memory_space=pltpu.SMEM)
    outside = pl.BlockSpec(memory_space=pl.ANY)
    targets = [
        pltpu.VMEM(array.shape if geometry or at < 2 else (width,) + array.shape[1:], array.dtype)
        for at, array in enumerate(used)
    ]

    def kernel(*refs):
        child_kernel(first, width, regions, slots, *refs)

    return pl.pallas_call(
        kernel,
        out_shape=(half, half),
        in_specs=[scalars, scalars] + [outside] * len(used),
        out_specs=(outside, outside),
        scratch_shapes=targets
        + [
            pltpu.VMEM((padded * block_count, row_count), jnp.float32),
            pltpu.VMEM((2 * regions * per_region, TILE, row_count), jnp.float32),
            pltpu.SemaphoreType.DMA((len(used),)),
            pltpu.SemaphoreType.DMA((2,)),
        ],
        compiler_params=pltpu.CompilerParams(vmem_limit_bytes=vmem * 1024 * 1024),
        cost_estimate=pl.CostEstimate(flops=1024, bytes_accessed=1024, transcendentals=0),
        name="fold_children",
    )(place, live, *used)


def group_sizes(widths, cap):
    full = sum(width // TILE for width in widths)
    extra = sum(width % TILE for width in widths)
    return full, extra, full * cap + (1 if extra else 0)


def parent_kernel(widths, owners, cap, coded, *refs):
    place_ref, code_ref, rows_ref = refs[:3]
    sums_refs = refs[3 : 3 + len(widths)]
    totals = refs[3 + len(widths)]
    block_count = rows_ref.shape[0]
    full, extra, used = group_sizes(widths, cap)
    per_owner = used + (1 if coded else 0)
    totals[...] = jnp.zeros(totals.shape, jnp.float32)
    for start in range(0, block_count, UNROLL):
        folded = []
        for block in range(start, start + UNROLL):
            place = place_ref[block]
            owner, rank = place // cap, place % cap
            lines, shared = [], []
            for width, sums_ref in zip(widths, sums_refs, strict=True):
                tiles = width // TILE
                lines += [sums_ref[tile * block_count + block] for tile in range(tiles)]
                if width % TILE:
                    share = TILE // extra
                    line = sums_ref[tiles * block_count + block // share]
                    line = spread_group(line, extra, block % share)
                    shared.append(jnp.where(tile_rows() // extra == rank, line, 0.0))
            rows = rows_ref[pl.ds(block, 1), :]
            result = fold_block(jnp.concatenate(lines + shared, 0), rows)
            folded.append((owner * per_owner, rank, result))
            if coded:
                code = code_ref[block].astype(jnp.float32)
                totals[owner * per_owner + used] += jnp.where(tile_rows() == rank, code, 0.0)
        for base, rank, result in folded:
            for tile in range(full):
                totals[base + tile * cap + rank] += result[tile * TILE : (tile + 1) * TILE]
            if extra:
                totals[base + full * cap] += result[full * TILE :]


def fold_parents(place, code, rows, sums, widths, owners, cap, coded):
    row_count = rows.shape[1]
    per_owner = group_sizes(widths, cap)[2] + (1 if coded else 0)
    whole = pl.BlockSpec(memory_space=pltpu.VMEM)
    scalars = pl.BlockSpec(memory_space=pltpu.SMEM)

    def kernel(*refs):
        parent_kernel(widths, owners, cap, coded, *refs)

    return pl.pallas_call(
        kernel,
        out_shape=jax.ShapeDtypeStruct((owners * per_owner, TILE, row_count), jnp.float32),
        in_specs=[scalars, scalars, whole] + [whole] * len(sums),
        out_specs=whole,
        compiler_params=pltpu.CompilerParams(vmem_limit_bytes=16 * 1024 * 1024),
        cost_estimate=pl.CostEstimate(flops=1024, bytes_accessed=1024, transcendentals=0),
        name="fold_parents",
    )(place, code, rows, *sums)


def place_kernel(widths, owners, cap, slots, coded, *refs):
    if coded:
        sub_ref, in_ref, keep_ref, send_ref, codes_ref = refs
    else:
        codes_in, in_ref, keep_ref, send_ref = refs
    full, extra, used = group_sizes(widths, cap)
    per_owner = used + (1 if coded else 0)
    if coded:
        for owner in range(owners):
            code = in_ref[owner * per_owner + used].astype(jnp.int32)
            codes_ref[owner] = (code // slots + sub_ref[0]) % 2 * slots + code % slots
        codes_in = codes_ref
    for half, out_ref in enumerate((keep_ref, send_ref)):
        for slot in range(slots):
            label = half * slots + slot
            sums = [jnp.zeros(in_ref.shape[1:], jnp.float32) for _ in range(full)]
            for owner in range(owners):
                for rank in range(cap):
                    here = codes_in[owner, rank : rank + 1, :] == label
                    for tile in range(full):
                        line = in_ref[owner * per_owner + tile * cap + rank]
                        sums[tile] += jnp.where(here, line, 0.0)
            for tile in range(full):
                out_ref[tile * slots + slot] = sums[tile]
        if extra:
            share = TILE // extra
            sums = [jnp.zeros(in_ref.shape[1:], jnp.float32) for _ in range(slots // share)]
            for owner in range(owners):
                for rank in range(cap):
                    line = spread_group(in_ref[owner * per_owner + full * cap], extra, rank)
                    code = codes_in[owner, rank : rank + 1, :] - half * slots - tile_rows() // extra
                    for tile in range(slots // share):
                        sums[tile] += jnp.where(code == tile * share, line, 0.0)
            for tile in range(slots // share):
                out_ref[full * slots + tile] = sums[tile]


def place_parents(sub_at, codes, received, widths, owners, cap, slots):
    row_count = received.shape[2]
    coded = codes is None
    full, extra, _ = group_sizes(widths, cap)
    per_half = full * slots + slots * extra // TILE
    whole = pl.BlockSpec(memory_space=pltpu.VMEM)
    scalars = pl.BlockSpec(memory_space=pltpu.SMEM)
    half = jax.ShapeDtypeStruct((per_half, TILE, row_count), jnp.float32)
    table = jax.ShapeDtypeStruct((owners, TILE, row_count), jnp.int32)

    def kernel(*refs):
        place_kernel(widths, owners, cap, slots, coded, *refs)

    return pl.pallas_call(
        kernel,
        out_shape=(half, half, table) if coded else (half, half),
        in_specs=[scalars if coded else whole, whole],
        out_specs=(whole, whole, whole) if coded else (whole, whole),
        compiler_params=pltpu.CompilerParams(vmem_limit_bytes=16 * 1024 * 1024),
        cost_estimate=pl.CostEstimate(flops=1024, bytes_accessed=1024, transcendentals=0),
        name="place_parents",
    )(sub_at.reshape(1) if coded else codes, received)


def unpack(tiles, widths, slots):
    row_count = tiles.shape[2]
    parts, start = [], 0
    for width in widths:
        full = width // TILE
        whole = tiles[start : start + full * slots].reshape(full, slots, TILE, row_count)
        parts.append([whole.transpose(0, 2, 1, 3).reshape(full * TILE, slots, row_count)])
        start += full * slots
    for part, width in zip(parts, widths, strict=True):
        if width % TILE:
            rest = tiles[start:].reshape(slots, width % TILE, row_count)
            part.append(rest.transpose(1, 0, 2))
    return [jnp.concatenate(part, 0) for part in parts]


def merged_parts(parts):
    sums = parts[0]
    divisor = jnp.maximum(sums[0], WEIGHT_FLOOR)
    centre = sums[1:4] / divisor
    centre_outer = jnp.stack([centre[first] * centre[second] for first, second in PAIRS])
    spread = sums[4:10] / divisor - centre_outer
    rest = [part / divisor for part in [sums[10:]] + parts[1:] if part.shape[0]]
    return jnp.concatenate([sums[:1], centre, spread] + rest, 0)


def cut_components(components):
    chunks, start = [(0, 10)], 10
    for width in WIDTHS:
        width = min(width, components - start)
        if width > 0:
            chunks.append((start, width))
            start += width
    if start < components:
        chunks.append((start, components - start))
    return chunks


def after(values, *others):
    return lax.optimization_barrier((values,) + others)[0]


def span_body(
    child_weight,
    child_mean,
    child_factor,
    child_colour,
    child_dest,
    child_slot,
    child_row,
    live_blocks,
    parent_owner,
    parent_slot,
    parent_row,
):
    spans = lax.axis_size("span")
    levels = spans.bit_length() - 1
    components = 10 + child_colour.shape[0]
    span_at, sub_at = lax.axis_index("span"), lax.axis_index("sub")
    cap_two = max(1, (PB_DEV + spans - 1) // spans)

    def swap(values):
        return lax.ppermute(values, "sub", [(0, 1), (1, 0)])

    def cross(values, bit):
        return lax.ppermute(values, "span", [(at, at ^ (1 << bit)) for at in range(spans)])

    away = child_dest ^ span_at
    half = (child_slot // PB_DEV + sub_at) % 2

    def place_in(order):
        region = sum(((away >> bit) & 1) << (levels - 1 - at) for at, bit in enumerate(order))
        return (half * spans + region) * PB_DEV + child_slot % PB_DEV

    place_two = parent_owner * cap_two + earlier_same(parent_owner)

    arrays = (child_row, child_weight, child_mean, child_factor, child_colour)
    chunks = cut_components(components)
    total = len(chunks)
    sizes = [tile_count(width, PB_DEV) for _, width in chunks]
    orders = [list(range(levels)) for _ in chunks]
    terms = [[] for _ in chunks]
    sends = [[] for _ in chunks]

    def fold(at, *others):
        place = place_in(orders[at])
        if others:
            place = after(place, *others)
        keep, send = fold_children(place, live_blocks, arrays, *chunks[at], spans, PB_DEV, 56 if at < HEAD else 40)
        terms[at] = [keep, swap(send)]

    def part(at, low, high):
        return sum(
            (term[low * sizes[at] : high * sizes[at]] for term in terms[at][1:]),
            start=terms[at][0][low * sizes[at] : high * sizes[at]],
        )

    def exchange(at, level, *others):
        low = spans >> (level + 1)
        send = part(at, low, 2 * low)
        if others:
            send = after(send, *others)
        sends[at].append(send)
        terms[at].append(cross(send, orders[at][level]))

    def send_of(at, level):
        low = spans >> (level + 1)
        return part(at, low, 2 * low)

    def depart(at, level, send):
        terms[at].append(cross(send, orders[at][level]))

    def depart_alone(at, level):
        send = send_of(at, level)
        depart(at, level, send)
        return send

    level_two, codes, fetched = [], [None], []

    def raise_level(group, *others):
        widths = [chunks[at][1] for at in group]
        parts = fold_parents(
            after(place_two, *others) if others else place_two,
            parent_slot,
            parent_row,
            [sums[at] for at in group],
            widths,
            spans,
            cap_two,
            codes[0] is None,
        )
        parts = lax.all_to_all(parts, "span", split_axis=0, concat_axis=0, tiled=True)
        fetched.append(parts)
        placed = place_parents(sub_at, codes[0], parts, widths, spans, cap_two, GB_DEV)
        if codes[0] is None:
            codes[0] = placed[2]
        level_two.extend(unpack(placed[0] + swap(placed[1]), widths, GB_DEV))

    fold(0)
    fold(1, terms[0][0])
    first_send = depart_alone(0, 0)
    fold(2, terms[1][0], first_send)
    second_send = depart_alone(1, 0)
    for at in range(3, total):
        fold(at, terms[at - 1][0], second_send)
    sums = [None] * total
    for phase in range(total + levels - 2):
        moves, done = [], []
        if phase + 2 < total:
            moves.append((phase + 2, 0))
        for turn in range(levels - 1):
            if 0 <= phase - turn < total:
                moves.append((phase - turn, turn + 1))
        if phase >= levels - 1:
            done.append(terms[phase - levels + 1][-1])
        if phase == 0:
            done.append(terms[total - 1][1])
        if WAIT_FETCH:
            done += fetched[-1:]
        ready = [send_of(at, level) for at, level in moves]
        ready = lax.optimization_barrier(tuple(ready + done))[: len(ready)]
        for (at, level), send in zip(moves, ready, strict=True):
            depart(at, level, send)
            if level == levels - 1:
                sums[at] = part(at, 0, 1)
        if phase in GROUPS:
            raise_level(GROUPS[phase], *ready)
    raise_level(GROUPS[total + levels - 2])
    level_one = []
    for at in range(total):
        level_one += unpack(sums[at], [chunks[at][1]], PB_DEV)
    return (merged_parts(level_one), merged_parts(level_two))


def body(*arrays):
    spans, subs = lax.axis_size("span"), lax.axis_size("sub")
    blocks = arrays[0].shape[0]
    dense = spans * subs * PB_DEV
    fits = subs == 2 and spans & (spans - 1) == 0 and dense <= 4 * blocks
    if fits and PB_DEV == 4 * spans and blocks % 16 == 0:
        return span_body(*arrays)
    return plain_body(*arrays)


def solution(mesh):
    placed = (
        P(("groups", "span", "sub"), None),
        P(None, ("groups", "span", "sub"), None),
        P(None, ("groups", "span", "sub"), None),
        P(None, ("groups", "span", "sub"), None),
        P(("groups", "span", "sub")),
        P(("groups", "span", "sub")),
        P(("groups", "span", "sub"), None),
        P(("groups", "span", "sub")),
        P(("groups", "span", "sub")),
        P(("groups", "span", "sub")),
        P(("groups", "span", "sub"), None),
    )
    return jax.shard_map(
        body,
        mesh=mesh,
        in_specs=placed,
        out_specs=(
            P(None, ("groups", "span", "sub"), None),
            P(None, ("groups", "span", "sub"), None),
        ),
        check_vma=False,
    )
```

```python
import math

import jax
import jax.numpy as jnp
from jax import lax
from jax.experimental import pallas as pl
from jax.experimental.pallas import tpu as pltpu
from jax.sharding import PartitionSpec as P

PB_DEV = 32
GB_DEV = 8


PAIRS = ((0, 0), (0, 1), (0, 2), (1, 1), (1, 2), (2, 2))
WEIGHT_FLOOR = 0.1


def covariance(factor):
    return jnp.stack(
        [
            factor[0] * factor[0],
            factor[0] * factor[1],
            factor[0] * factor[3],
            factor[1] * factor[1] + factor[2] * factor[2],
            factor[1] * factor[3] + factor[2] * factor[4],
            factor[3] * factor[3] + factor[4] * factor[4] + factor[5] * factor[5],
        ]
    )


def moment_sums(weight, centres, factor, colour):
    outer = jnp.stack([centres[first] * centres[second] for first, second in PAIRS])
    return jnp.concatenate(
        [
            weight[None],
            weight * centres,
            weight * (covariance(factor) + outer),
            weight * colour.astype(jnp.float32),
        ],
        0,
    )


def match_moments(sums):
    whole_weight = sums[0]
    divisor = jnp.maximum(whole_weight, WEIGHT_FLOOR)
    centre = sums[1:4] / divisor
    centre_outer = jnp.stack([centre[first] * centre[second] for first, second in PAIRS])
    spread = sums[4:10] / divisor - centre_outer
    colour_mean = sums[10:] / divisor
    return jnp.concatenate([whole_weight[None], centre, spread, colour_mean], 0)


def earlier_same(owners):
    position = jnp.arange(owners.shape[0], dtype=jnp.int32)
    same_owner = (owners[:, None] == owners[None, :]) & (position[None, :] < position[:, None])
    return jnp.sum(same_owner.astype(jnp.int32), 1)


def fold_rows(values, row_picks):
    block_total = values.shape[1]
    width = values.shape[2]
    group_size = math.gcd(block_total, 16)
    row_labels = jnp.arange(width, dtype=jnp.int32)

    def fold_step(turn_index, result):
        start = turn_index * group_size
        block_part = lax.dynamic_slice_in_dim(values, start, group_size, 1)
        picks_part = lax.dynamic_slice_in_dim(row_picks, start, group_size, 0)
        row_table = (picks_part[:, :, None] == row_labels).astype(jnp.float32)
        folded_part = jnp.einsum(
            "cbr,brj->cbj", block_part, row_table, precision=lax.Precision.HIGHEST
        )
        return lax.dynamic_update_slice_in_dim(result, folded_part, start, 1)

    return lax.fori_loop(
        0, block_total // group_size, fold_step, jnp.zeros(values.shape, jnp.float32)
    )


def place_blocks(values, block_picks, block_count):
    block_table = (block_picks[:, None] == jnp.arange(block_count, dtype=jnp.int32)).astype(
        jnp.float32
    )
    return jnp.einsum("csj,sp->cpj", values, block_table, precision=lax.Precision.HIGHEST)


def seam(partial_value, per_device):
    whole_sum = lax.psum(partial_value, "sub")
    return lax.dynamic_slice_in_dim(whole_sum, lax.axis_index("sub") * per_device, per_device, 1)


def plain_body(
    child_weight,
    child_mean,
    child_factor,
    child_colour,
    child_dest,
    child_slot,
    child_row,
    live_blocks,
    parent_owner,
    parent_slot,
    parent_row,
):
    spans = lax.axis_size("span")
    sub_count = lax.axis_size("sub")
    block_count = child_weight.shape[0]
    row_count = child_weight.shape[1]
    components = 10 + child_colour.shape[0]
    cap_one = max(2, (2 * block_count + spans - 1) // spans)
    slot_total = spans * cap_one
    parent_span = PB_DEV * sub_count
    moments = moment_sums(child_weight, child_mean, child_factor, child_colour)
    position = jnp.arange(block_count, dtype=jnp.int32)
    is_live = position < live_blocks[0]
    slot_index = jnp.where(is_live, child_dest * cap_one + earlier_same(child_dest), slot_total)
    outgoing_shape = (components, slot_total, row_count)
    outgoing = jnp.zeros(outgoing_shape, jnp.float32).at[:, slot_index].set(moments, mode="drop")
    targets = child_slot[:, None] * row_count + child_row
    target_rows = (
        jnp.zeros((1, slot_total, row_count), jnp.int32).at[0, slot_index].set(targets, mode="drop")
    )
    received, received_rows = (
        lax.all_to_all(outgoing, "span", split_axis=1, concat_axis=1, tiled=True),
        lax.all_to_all(target_rows, "span", split_axis=1, concat_axis=1, tiled=True),
    )
    incoming_rows = received_rows[0]
    folded = fold_rows(received, incoming_rows % row_count)
    collected = place_blocks(folded, incoming_rows[:, 0] // row_count, parent_span)
    own_sums = seam(collected, PB_DEV)
    level_one = match_moments(own_sums)
    cap_two = max(1, (PB_DEV + spans - 1) // spans)
    slot_two = parent_owner * cap_two + earlier_same(parent_owner)
    outgoing_two = (
        jnp.zeros((components, spans * cap_two, row_count), jnp.float32)
        .at[:, slot_two]
        .set(own_sums)
    )
    targets_two = parent_slot[:, None] * row_count + parent_row
    rows_two = (
        jnp.zeros((1, spans * cap_two, row_count), jnp.int32).at[0, slot_two].set(targets_two)
    )
    received_two, received_rows_two = (
        lax.all_to_all(outgoing_two, "span", split_axis=1, concat_axis=1, tiled=True),
        lax.all_to_all(rows_two, "span", split_axis=1, concat_axis=1, tiled=True),
    )
    grand_span = GB_DEV * sub_count
    incoming_two = received_rows_two[0]
    folded_two = fold_rows(received_two, incoming_two % row_count)
    collected_two = place_blocks(folded_two, incoming_two[:, 0] // row_count, grand_span)
    level_two = match_moments(seam(collected_two, GB_DEV))
    return (level_one, level_two)


TILE = 8
UNROLL = 8
WIDTHS = (8, 8, 8, 8, 8, 8)
FOLDS = ((0,), (1, 2, 3), (4, 5, 6))
GROUPS = {8: (0, 1, 2, 3, 4, 5, 6)}
WAIT_FETCH = False
LOOSE = -9
EARLY_ONE = True
PHASE0 = False
TIES = 1
HEAD = 1


def tile_count(width, slots):
    return (width // TILE) * slots + (slots * (width % TILE) + TILE - 1) // TILE


def split_pair(values):
    high = values.astype(jnp.bfloat16)
    low = (values - high.astype(jnp.float32)).astype(jnp.bfloat16)
    return jnp.concatenate([high, low], 1)


def row_table(rows):
    width = rows.shape[1]
    labels = lax.broadcasted_iota(jnp.int32, (width, width), 0)
    picks = jnp.where(labels == rows, 1.0, 0.0).astype(jnp.bfloat16)
    return jnp.concatenate([picks, picks], 1)


def fold_block(values, rows):
    return lax.dot_general(
        split_pair(values),
        row_table(rows),
        (((1,), (1,)), ((), ())),
        preferred_element_type=jnp.float32,
    )


def tile_rows():
    return lax.broadcasted_iota(jnp.int32, (TILE, 1), 0)


def spread_group(line, extra, group):
    share = TILE // extra
    line = jnp.where(tile_rows() // extra == group, line, 0.0)
    return sum((pltpu.roll(line, turn * extra, 0) for turn in range(1, share)), start=line)


def child_kernel(first, widths, regions, slots, *refs):
    geometry = first == 0
    place_ref, live_ref = refs[:2]
    count = 4 if geometry else 3
    sources = refs[2 : 2 + count]
    refs = refs[2 + count :]
    out_refs, refs = refs[: 2 * len(widths)], refs[2 * len(widths) :]
    targets = refs[:count]
    rows_ref, weight_ref = targets[:2]
    moments, totals, load_sems, out_sems = refs[count:]
    block_count, row_count = rows_ref.shape
    width = sum(widths)
    full, extra = width // TILE, width % TILE
    sizes = [tile_count(part, slots) for part in widths]
    starts = [2 * regions * sum(sizes[:at]) for at in range(len(sizes))]
    tiles = [(at, tile) for at, part in enumerate(widths) for tile in range(part // TILE)]
    group = 16
    first_colour = max(first, 10) - 10
    colour_total = 0 if geometry else width
    loads = []
    for at, (source, target) in enumerate(zip(sources, targets, strict=True)):
        if colour_total and at == 2:
            source = source.at[pl.ds(first_colour, colour_total)]
        loads.append(pltpu.make_async_copy(source, target, load_sems.at[at]))
    if geometry:
        mean_ref, factor_ref = targets[2:4]
    else:
        colours = targets[2]
    for load in loads:
        load.start()

    def clear(step, carry):
        totals[pl.ds(step * 16, 16)] = jnp.zeros((16, TILE, row_count), jnp.float32)
        return carry

    lax.fori_loop(0, totals.shape[0] // 16, clear, 0)
    for load in loads:
        load.wait()

    def prepare(step, carry):
        start = pl.multiple_of(step * group, group)
        part = pl.ds(start, group)
        weight = weight_ref[part, :]
        values = {}
        if geometry:
            centre = [mean_ref[axis, part, :] for axis in range(3)]
            factor = [factor_ref[entry, part, :] for entry in range(6)]
            spread = [
                factor[0] * factor[0],
                factor[0] * factor[1],
                factor[0] * factor[3],
                factor[1] * factor[1] + factor[2] * factor[2],
                factor[1] * factor[3] + factor[2] * factor[4],
                factor[3] * factor[3] + factor[4] * factor[4] + factor[5] * factor[5],
            ]
            values[0] = weight
            for axis in range(3):
                values[1 + axis] = weight * centre[axis]
            for entry, (left, right) in enumerate(PAIRS):
                values[4 + entry] = weight * (spread[entry] + centre[left] * centre[right])
        for entry in range(colour_total):
            values[10 + first_colour + entry] = weight * colours[entry, part, :].astype(jnp.float32)
        for place in range(full * TILE + (TILE if extra else 0)):
            component = first + (place if place < full * TILE else full * TILE + place % extra)
            moments[pl.ds(place * block_count + start, group), :] = values[component]
        return carry

    lax.fori_loop(0, block_count // group, prepare, 0)
    live = live_ref[0]

    def fold(step, carry):
        folded = []
        for turn in range(UNROLL):
            block = step * UNROLL + turn
            place = place_ref[block]
            region, slot = place // slots, place % slots
            lines = [
                moments[pl.ds(tile * TILE * block_count + block, TILE, stride=block_count), :]
                for tile in range(full)
            ]
            if extra:
                line = moments[pl.ds(full * TILE * block_count + block, TILE, stride=block_count), :]
                lines.append(jnp.where(tile_rows() // extra == slot % (TILE // extra), line, 0.0))
            rows = jnp.where(block < live, rows_ref[pl.ds(block, 1), :], -1)
            folded.append((region, slot, fold_block(jnp.concatenate(lines, 0), rows)))
        for region, slot, result in folded:
            for line, (at, tile) in enumerate(tiles):
                spot = starts[at] + region * sizes[at] + tile * slots + slot
                totals[spot] += result[line * TILE : (line + 1) * TILE]
            if extra:
                spot = starts[-1] + region * sizes[-1] + (widths[-1] // TILE) * slots
                totals[spot + slot // (TILE // extra)] += result[full * TILE :]
        return carry

    lax.fori_loop(0, (live + UNROLL - 1) // UNROLL, fold, 0)
    stores = []
    for at, size in enumerate(sizes):
        half = regions * size
        for turn in (1, 0):
            source = totals.at[pl.ds(starts[at] + turn * half, half)]
            store = pltpu.make_async_copy(source, out_refs[2 * at + turn], out_sems.at[2 * at + turn])
            store.start()
            stores.append(store)
    for store in stores:
        store.wait()


def fold_children(place, live, arrays, first, widths, regions, slots, vmem):
    rows, weight, mean, factor, colour = arrays
    geometry = first == 0
    used = [rows, weight, mean, factor] if geometry else [rows, weight, colour]
    block_count, row_count = rows.shape
    width = sum(widths)
    sizes = [tile_count(part, slots) for part in widths]
    padded = width // TILE * TILE + (TILE if width % TILE else 0)
    halves = [
        jax.ShapeDtypeStruct((regions * size, TILE, row_count), jnp.float32)
        for size in sizes
        for _ in range(2)
    ]
    scalars = pl.BlockSpec(memory_space=pltpu.SMEM)
    outside = pl.BlockSpec(memory_space=pl.ANY)
    targets = [
        pltpu.VMEM(array.shape if geometry or at < 2 else (width,) + array.shape[1:], array.dtype)
        for at, array in enumerate(used)
    ]

    def kernel(*refs):
        child_kernel(first, widths, regions, slots, *refs)

    return pl.pallas_call(
        kernel,
        out_shape=halves,
        in_specs=[scalars, scalars] + [outside] * len(used),
        out_specs=[outside] * len(halves),
        scratch_shapes=targets
        + [
            pltpu.VMEM((padded * block_count, row_count), jnp.float32),
            pltpu.VMEM((2 * regions * sum(sizes), TILE, row_count), jnp.float32),
            pltpu.SemaphoreType.DMA((len(used),)),
            pltpu.SemaphoreType.DMA((len(halves),)),
        ],
        compiler_params=pltpu.CompilerParams(vmem_limit_bytes=vmem * 1024 * 1024),
        cost_estimate=pl.CostEstimate(flops=1024, bytes_accessed=1024, transcendentals=0),
        name="fold_children",
    )(place, live, *used)


def group_sizes(widths, cap):
    full = sum(width // TILE for width in widths)
    extra = sum(width % TILE for width in widths)
    return full, extra, full * cap + (1 if extra else 0)


def parent_kernel(widths, owners, cap, coded, *refs):
    place_ref, code_ref, rows_ref = refs[:3]
    sums_refs = refs[3 : 3 + len(widths)]
    out_refs, totals = refs[3 + len(widths) : -1], refs[-1]
    block_count = rows_ref.shape[0]
    full, extra, used = group_sizes(widths, cap)
    per_owner = used + (1 if coded else 0)
    totals[...] = jnp.zeros(totals.shape, jnp.float32)
    for start in range(0, block_count, UNROLL):
        folded = []
        for block in range(start, start + UNROLL):
            place = place_ref[block]
            owner, rank = place // cap, place % cap
            lines, shared = [], []
            for width, sums_ref in zip(widths, sums_refs, strict=True):
                tiles = width // TILE
                lines += [sums_ref[tile * block_count + block] for tile in range(tiles)]
                if width % TILE:
                    share = TILE // extra
                    line = sums_ref[tiles * block_count + block // share]
                    line = spread_group(line, extra, block % share)
                    shared.append(jnp.where(tile_rows() // extra == rank, line, 0.0))
            rows = rows_ref[pl.ds(block, 1), :]
            result = fold_block(jnp.concatenate(lines + shared, 0), rows)
            folded.append((owner * per_owner, rank, result))
            if coded:
                code = code_ref[block].astype(jnp.float32)
                totals[owner * per_owner + used] += jnp.where(tile_rows() == rank, code, 0.0)
        for base, rank, result in folded:
            for tile in range(full):
                totals[base + tile * cap + rank] += result[tile * TILE : (tile + 1) * TILE]
            if extra:
                totals[base + full * cap] += result[full * TILE :]
    for owner, out_ref in enumerate(out_refs):
        out_ref[...] = totals[owner * per_owner : (owner + 1) * per_owner]


def fold_parents(place, code, rows, sums, widths, owners, cap, coded):
    row_count = rows.shape[1]
    per_owner = group_sizes(widths, cap)[2] + (1 if coded else 0)
    whole = pl.BlockSpec(memory_space=pltpu.VMEM)
    scalars = pl.BlockSpec(memory_space=pltpu.SMEM)

    def kernel(*refs):
        parent_kernel(widths, owners, cap, coded, *refs)

    return pl.pallas_call(
        kernel,
        out_shape=[jax.ShapeDtypeStruct((per_owner, TILE, row_count), jnp.float32)] * owners,
        in_specs=[scalars, scalars, whole] + [whole] * len(sums),
        out_specs=[whole] * owners,
        scratch_shapes=[pltpu.VMEM((owners * per_owner, TILE, row_count), jnp.float32)],
        compiler_params=pltpu.CompilerParams(vmem_limit_bytes=16 * 1024 * 1024),
        cost_estimate=pl.CostEstimate(flops=1024, bytes_accessed=1024, transcendentals=0),
        name="fold_parents",
    )(place, code, rows, *sums)


def place_kernel(widths, owners, cap, slots, coded, *refs):
    first_ref, in_refs, out_refs = refs[0], refs[1 : 1 + owners], refs[1 + owners :]
    keep_ref, send_ref = out_refs[:2]
    shape = in_refs[0].shape[1:]
    full, extra, used = group_sizes(widths, cap)
    if coded:
        for owner in range(owners):
            code = in_refs[owner][used].astype(jnp.int32)
            out_refs[2][owner] = (code // slots + first_ref[0]) % 2 * slots + code % slots
    codes_in = out_refs[2] if coded else first_ref
    for half, out_ref in enumerate((keep_ref, send_ref)):
        for slot in range(slots):
            label = half * slots + slot
            sums = [jnp.zeros(shape, jnp.float32) for _ in range(full)]
            for owner in range(owners):
                for rank in range(cap):
                    here = codes_in[owner, rank : rank + 1, :] == label
                    for tile in range(full):
                        line = in_refs[owner][tile * cap + rank]
                        sums[tile] += jnp.where(here, line, 0.0)
            for tile in range(full):
                out_ref[tile * slots + slot] = sums[tile]
        if extra:
            share = TILE // extra
            sums = [jnp.zeros(shape, jnp.float32) for _ in range(slots // share)]
            for owner in range(owners):
                for rank in range(cap):
                    line = spread_group(in_refs[owner][full * cap], extra, rank)
                    code = codes_in[owner, rank : rank + 1, :] - half * slots - tile_rows() // extra
                    for tile in range(slots // share):
                        sums[tile] += jnp.where(code == tile * share, line, 0.0)
            for tile in range(slots // share):
                out_ref[full * slots + tile] = sums[tile]


def place_parents(sub_at, codes, received, widths, owners, cap, slots):
    row_count = received[0].shape[2]
    coded = codes is None
    full, extra, _ = group_sizes(widths, cap)
    per_half = full * slots + slots * extra // TILE
    whole = pl.BlockSpec(memory_space=pltpu.VMEM)
    scalars = pl.BlockSpec(memory_space=pltpu.SMEM)
    half = jax.ShapeDtypeStruct((per_half, TILE, row_count), jnp.float32)
    table = jax.ShapeDtypeStruct((owners, TILE, row_count), jnp.int32)

    def kernel(*refs):
        place_kernel(widths, owners, cap, slots, coded, *refs)

    return pl.pallas_call(
        kernel,
        out_shape=(half, half, table) if coded else (half, half),
        in_specs=[scalars if coded else whole] + [whole] * owners,
        out_specs=(whole, whole, whole) if coded else (whole, whole),
        compiler_params=pltpu.CompilerParams(vmem_limit_bytes=16 * 1024 * 1024),
        cost_estimate=pl.CostEstimate(flops=1024, bytes_accessed=1024, transcendentals=0),
        name="place_parents",
    )(sub_at.reshape(1) if coded else codes, *received)


def unpack(tiles, widths, slots):
    row_count = tiles.shape[2]
    parts, start = [], 0
    for width in widths:
        full = width // TILE
        whole = tiles[start : start + full * slots].reshape(full, slots, TILE, row_count)
        parts.append([whole.transpose(0, 2, 1, 3).reshape(full * TILE, slots, row_count)])
        start += full * slots
    for part, width in zip(parts, widths, strict=True):
        if width % TILE:
            rest = tiles[start:].reshape(slots, width % TILE, row_count)
            part.append(rest.transpose(1, 0, 2))
    return [jnp.concatenate(part, 0) for part in parts]


def merged_parts(parts):
    sums = parts[0]
    divisor = jnp.maximum(sums[0], WEIGHT_FLOOR)
    centre = sums[1:4] / divisor
    centre_outer = jnp.stack([centre[first] * centre[second] for first, second in PAIRS])
    spread = sums[4:10] / divisor - centre_outer
    rest = [part / divisor for part in [sums[10:]] + parts[1:] if part.shape[0]]
    return jnp.concatenate([sums[:1], centre, spread] + rest, 0)


def cut_components(components):
    chunks, start = [(0, 10)], 10
    for width in WIDTHS:
        width = min(width, components - start)
        if width > 0:
            chunks.append((start, width))
            start += width
    if start < components:
        chunks.append((start, components - start))
    return chunks


def after(values, *others):
    return lax.optimization_barrier((values,) + others)[0]


def span_body(
    child_weight,
    child_mean,
    child_factor,
    child_colour,
    child_dest,
    child_slot,
    child_row,
    live_blocks,
    parent_owner,
    parent_slot,
    parent_row,
):
    spans = lax.axis_size("span")
    levels = spans.bit_length() - 1
    components = 10 + child_colour.shape[0]
    span_at, sub_at = lax.axis_index("span"), lax.axis_index("sub")
    cap_two = max(1, (PB_DEV + spans - 1) // spans)

    def swap(values):
        return lax.ppermute(values, "sub", [(0, 1), (1, 0)])

    def cross(values, bit):
        return lax.ppermute(values, "span", [(at, at ^ (1 << bit)) for at in range(spans)])

    away = child_dest ^ span_at
    half = (child_slot // PB_DEV + sub_at) % 2

    def place_in(order):
        region = sum(((away >> bit) & 1) << (levels - 1 - at) for at, bit in enumerate(order))
        return (half * spans + region) * PB_DEV + child_slot % PB_DEV

    place_two = (parent_owner ^ span_at) * cap_two + earlier_same(parent_owner)

    arrays = (child_row, child_weight, child_mean, child_factor, child_colour)
    chunks = cut_components(components)
    total = len(chunks)
    sizes = [tile_count(width, PB_DEV) for _, width in chunks]
    orders = [list(range(levels)) for _ in chunks]
    terms = [[] for _ in chunks]
    sends = [[] for _ in chunks]

    def fold(group, *others):
        place = place_in(orders[group[0]])
        if others:
            place = after(place, *others)
        widths = [chunks[at][1] for at in group]
        vmem = 56 if group[0] < HEAD else 40
        halves = fold_children(
            place, live_blocks, arrays, chunks[group[0]][0], widths, spans, PB_DEV, vmem
        )
        for turn, at in enumerate(group):
            terms[at] = [halves[2 * turn], swap(halves[2 * turn + 1])]

    def part(at, low, high):
        return sum(
            (term[low * sizes[at] : high * sizes[at]] for term in terms[at][1:]),
            start=terms[at][0][low * sizes[at] : high * sizes[at]],
        )

    def exchange(at, level, *others):
        low = spans >> (level + 1)
        send = part(at, low, 2 * low)
        if others:
            send = after(send, *others)
        sends[at].append(send)
        terms[at].append(cross(send, orders[at][level]))

    def send_of(at, level):
        low = spans >> (level + 1)
        return part(at, low, 2 * low)

    def depart(at, level, send):
        terms[at].append(cross(send, orders[at][level]))

    def depart_alone(at, level):
        send = send_of(at, level)
        depart(at, level, send)
        return send

    level_one, level_two, codes, fetched = [], [], [None], []

    def unpack_one():
        return [
            unpack(sums[at], [width], PB_DEV)[0] for at, (_, width) in enumerate(chunks)
        ]


    def raise_level(group, *others):
        widths = [chunks[at][1] for at in group]
        parts = fold_parents(
            after(place_two, *others) if others else place_two,
            parent_slot,
            parent_row,
            [sums[at] for at in group],
            widths,
            spans,
            cap_two,
            codes[0] is None,
        )
        parts = [
            lax.ppermute(part, "span", [(at, at ^ away) for at in range(spans)]) if away else part
            for away, part in enumerate(parts)
        ]
        fetched.append(parts[-1])
        if EARLY_ONE and group[-1] == total - 1:
            level_one.append(merged_parts(unpack_one()))
            parts = [after(part, level_one[0]) for part in parts]
        placed = place_parents(sub_at, codes[0], parts, widths, spans, cap_two, GB_DEV)
        if codes[0] is None:
            codes[0] = placed[2]
        level_two.extend(unpack(placed[0] + swap(placed[1]), widths, GB_DEV))

    fold(FOLDS[0])
    fold(FOLDS[1], terms[FOLDS[0][0]][0])
    ready_sends = [depart_alone(at, 0) for at in range(2)]
    for turn in range(2, len(FOLDS)):
        fold(FOLDS[turn], terms[FOLDS[turn - 1][0]][0], *ready_sends[: turn - 1 + TIES])
    sums = [None] * total
    for phase in range(total + levels - 2):
        moves, done = [], []
        if phase + 2 < total:
            moves.append((phase + 2, 0))
        for turn in range(levels - 1):
            if 0 <= phase - turn < total:
                moves.append((phase - turn, turn + 1))
        if phase >= levels - 1:
            done.append(terms[phase - levels + 1][-1])
        if phase == 0 and PHASE0:
            done.append(terms[total - 1][1])
        if WAIT_FETCH:
            done += fetched[-1:]
        ready = [send_of(at, level) for at, level in moves]
        if phase < total - LOOSE:
            ready = lax.optimization_barrier(tuple(ready + done))[: len(ready)]
        for (at, level), send in zip(moves, ready, strict=True):
            depart(at, level, send)
            if level == levels - 1:
                sums[at] = part(at, 0, 1)
        if phase in GROUPS:
            raise_level(GROUPS[phase], *ready)
    raise_level(GROUPS[total + levels - 2])
    return (level_one[0] if level_one else merged_parts(unpack_one()), merged_parts(level_two))


def body(*arrays):
    spans, subs = lax.axis_size("span"), lax.axis_size("sub")
    blocks = arrays[0].shape[0]
    dense = spans * subs * PB_DEV
    fits = subs == 2 and spans & (spans - 1) == 0 and dense <= 4 * blocks
    if fits and PB_DEV == 4 * spans and blocks % 16 == 0:
        return span_body(*arrays)
    return plain_body(*arrays)


def solution(mesh):
    placed = (
        P(("groups", "span", "sub"), None),
        P(None, ("groups", "span", "sub"), None),
        P(None, ("groups", "span", "sub"), None),
        P(None, ("groups", "span", "sub"), None),
        P(("groups", "span", "sub")),
        P(("groups", "span", "sub")),
        P(("groups", "span", "sub"), None),
        P(("groups", "span", "sub")),
        P(("groups", "span", "sub")),
        P(("groups", "span", "sub")),
        P(("groups", "span", "sub"), None),
    )
    return jax.shard_map(
        body,
        mesh=mesh,
        in_specs=placed,
        out_specs=(
            P(None, ("groups", "span", "sub"), None),
            P(None, ("groups", "span", "sub"), None),
        ),
        check_vma=False,
    )
```

```python
import math

import jax
import jax.numpy as jnp
from jax import lax
from jax.experimental import pallas as pl
from jax.experimental.pallas import tpu as pltpu
from jax.sharding import PartitionSpec as P

PB_DEV = 32
GB_DEV = 8


PAIRS = ((0, 0), (0, 1), (0, 2), (1, 1), (1, 2), (2, 2))
WEIGHT_FLOOR = 0.1


def covariance(factor):
    return jnp.stack(
        [
            factor[0] * factor[0],
            factor[0] * factor[1],
            factor[0] * factor[3],
            factor[1] * factor[1] + factor[2] * factor[2],
            factor[1] * factor[3] + factor[2] * factor[4],
            factor[3] * factor[3] + factor[4] * factor[4] + factor[5] * factor[5],
        ]
    )


def moment_sums(weight, centres, factor, colour):
    outer = jnp.stack([centres[first] * centres[second] for first, second in PAIRS])
    return jnp.concatenate(
        [
            weight[None],
            weight * centres,
            weight * (covariance(factor) + outer),
            weight * colour.astype(jnp.float32),
        ],
        0,
    )


def match_moments(sums):
    whole_weight = sums[0]
    divisor = jnp.maximum(whole_weight, WEIGHT_FLOOR)
    centre = sums[1:4] / divisor
    centre_outer = jnp.stack([centre[first] * centre[second] for first, second in PAIRS])
    spread = sums[4:10] / divisor - centre_outer
    colour_mean = sums[10:] / divisor
    return jnp.concatenate([whole_weight[None], centre, spread, colour_mean], 0)


def earlier_same(owners):
    position = jnp.arange(owners.shape[0], dtype=jnp.int32)
    same_owner = (owners[:, None] == owners[None, :]) & (position[None, :] < position[:, None])
    return jnp.sum(same_owner.astype(jnp.int32), 1)


def fold_rows(values, row_picks):
    block_total = values.shape[1]
    width = values.shape[2]
    group_size = math.gcd(block_total, 16)
    row_labels = jnp.arange(width, dtype=jnp.int32)

    def fold_step(turn_index, result):
        start = turn_index * group_size
        block_part = lax.dynamic_slice_in_dim(values, start, group_size, 1)
        picks_part = lax.dynamic_slice_in_dim(row_picks, start, group_size, 0)
        row_table = (picks_part[:, :, None] == row_labels).astype(jnp.float32)
        folded_part = jnp.einsum(
            "cbr,brj->cbj", block_part, row_table, precision=lax.Precision.HIGHEST
        )
        return lax.dynamic_update_slice_in_dim(result, folded_part, start, 1)

    return lax.fori_loop(
        0, block_total // group_size, fold_step, jnp.zeros(values.shape, jnp.float32)
    )


def place_blocks(values, block_picks, block_count):
    block_table = (block_picks[:, None] == jnp.arange(block_count, dtype=jnp.int32)).astype(
        jnp.float32
    )
    return jnp.einsum("csj,sp->cpj", values, block_table, precision=lax.Precision.HIGHEST)


def seam(partial_value, per_device):
    whole_sum = lax.psum(partial_value, "sub")
    return lax.dynamic_slice_in_dim(whole_sum, lax.axis_index("sub") * per_device, per_device, 1)


def plain_body(
    child_weight,
    child_mean,
    child_factor,
    child_colour,
    child_dest,
    child_slot,
    child_row,
    live_blocks,
    parent_owner,
    parent_slot,
    parent_row,
):
    spans = lax.axis_size("span")
    sub_count = lax.axis_size("sub")
    block_count = child_weight.shape[0]
    row_count = child_weight.shape[1]
    components = 10 + child_colour.shape[0]
    cap_one = max(2, (2 * block_count + spans - 1) // spans)
    slot_total = spans * cap_one
    parent_span = PB_DEV * sub_count
    moments = moment_sums(child_weight, child_mean, child_factor, child_colour)
    position = jnp.arange(block_count, dtype=jnp.int32)
    is_live = position < live_blocks[0]
    slot_index = jnp.where(is_live, child_dest * cap_one + earlier_same(child_dest), slot_total)
    outgoing_shape = (components, slot_total, row_count)
    outgoing = jnp.zeros(outgoing_shape, jnp.float32).at[:, slot_index].set(moments, mode="drop")
    targets = child_slot[:, None] * row_count + child_row
    target_rows = (
        jnp.zeros((1, slot_total, row_count), jnp.int32).at[0, slot_index].set(targets, mode="drop")
    )
    received, received_rows = (
        lax.all_to_all(outgoing, "span", split_axis=1, concat_axis=1, tiled=True),
        lax.all_to_all(target_rows, "span", split_axis=1, concat_axis=1, tiled=True),
    )
    incoming_rows = received_rows[0]
    folded = fold_rows(received, incoming_rows % row_count)
    collected = place_blocks(folded, incoming_rows[:, 0] // row_count, parent_span)
    own_sums = seam(collected, PB_DEV)
    level_one = match_moments(own_sums)
    cap_two = max(1, (PB_DEV + spans - 1) // spans)
    slot_two = parent_owner * cap_two + earlier_same(parent_owner)
    outgoing_two = (
        jnp.zeros((components, spans * cap_two, row_count), jnp.float32)
        .at[:, slot_two]
        .set(own_sums)
    )
    targets_two = parent_slot[:, None] * row_count + parent_row
    rows_two = (
        jnp.zeros((1, spans * cap_two, row_count), jnp.int32).at[0, slot_two].set(targets_two)
    )
    received_two, received_rows_two = (
        lax.all_to_all(outgoing_two, "span", split_axis=1, concat_axis=1, tiled=True),
        lax.all_to_all(rows_two, "span", split_axis=1, concat_axis=1, tiled=True),
    )
    grand_span = GB_DEV * sub_count
    incoming_two = received_rows_two[0]
    folded_two = fold_rows(received_two, incoming_two % row_count)
    collected_two = place_blocks(folded_two, incoming_two[:, 0] // row_count, grand_span)
    level_two = match_moments(seam(collected_two, GB_DEV))
    return (level_one, level_two)


TILE = 8
UNROLL = 8
WIDTHS = (8, 8, 8, 8, 8, 8)
LINE_FIRST = {0: 1, 3: 2}


def tile_count(width, slots):
    return (width // TILE) * slots + (slots * (width % TILE) + TILE - 1) // TILE


def split_pair(values):
    high = values.astype(jnp.bfloat16)
    low = (values - high.astype(jnp.float32)).astype(jnp.bfloat16)
    return jnp.concatenate([high, low], 1)


def row_table(rows):
    width = rows.shape[1]
    labels = lax.broadcasted_iota(jnp.int32, (width, width), 0)
    picks = jnp.where(labels == rows, 1.0, 0.0).astype(jnp.bfloat16)
    return jnp.concatenate([picks, picks], 1)


def fold_block(values, rows):
    return lax.dot_general(
        split_pair(values),
        row_table(rows),
        (((1,), (1,)), ((), ())),
        preferred_element_type=jnp.float32,
    )


def tile_rows():
    return lax.broadcasted_iota(jnp.int32, (TILE, 1), 0)


def spread_group(line, extra, group):
    share = TILE // extra
    line = jnp.where(tile_rows() // extra == group, line, 0.0)
    return sum((pltpu.roll(line, turn * extra, 0) for turn in range(1, share)), start=line)


def child_kernel(first, widths, regions, slots, *refs):
    geometry = first == 0
    colour_total = max(first + sum(widths) - max(first, 10), 0)
    place_ref, live_ref = refs[:2]
    count = 2 + 2 * geometry + (colour_total > 0)
    sources = refs[2 : 2 + count]
    refs = refs[2 + count :]
    out_refs, refs = refs[: 2 * len(widths)], refs[2 * len(widths) :]
    targets = refs[:count]
    rows_ref, weight_ref = targets[:2]
    moments, totals, load_sems, out_sems = refs[count:]
    block_count, row_count = rows_ref.shape
    width = sum(widths)
    sizes = [tile_count(part, slots) for part in widths]
    starts = [2 * regions * sum(sizes[:at]) for at in range(len(sizes))]
    tiles = [(at, tile) for at, part in enumerate(widths) for tile in range(part // TILE)]
    bases = [first + sum(widths[:at]) for at in range(len(widths))]
    components = [bases[at] + tile * TILE + line for at, tile in tiles for line in range(TILE)]
    full, extra = len(tiles), 0
    for at, part in enumerate(widths):
        if part % TILE:
            extra, shared = part % TILE, at
            components += [bases[at] + part - extra + line % extra for line in range(TILE)]
    group = 16
    first_colour = max(first, 10) - 10
    loads = []
    for at, (source, target) in enumerate(zip(sources, targets, strict=True)):
        if colour_total and at == count - 1:
            source = source.at[pl.ds(first_colour, colour_total)]
        loads.append(pltpu.make_async_copy(source, target, load_sems.at[at]))
    if geometry:
        mean_ref, factor_ref = targets[2:4]
    colours = targets[-1]
    for load in loads:
        load.start()

    def clear(step, carry):
        totals[pl.ds(step * 16, 16)] = jnp.zeros((16, TILE, row_count), jnp.float32)
        return carry

    lax.fori_loop(0, totals.shape[0] // 16, clear, 0)
    for load in loads:
        load.wait()

    def prepare(step, carry):
        start = pl.multiple_of(step * group, group)
        part = pl.ds(start, group)
        weight = weight_ref[part, :]
        values = {}
        if geometry:
            centre = [mean_ref[axis, part, :] for axis in range(3)]
            factor = [factor_ref[entry, part, :] for entry in range(6)]
            spread = [
                factor[0] * factor[0],
                factor[0] * factor[1],
                factor[0] * factor[3],
                factor[1] * factor[1] + factor[2] * factor[2],
                factor[1] * factor[3] + factor[2] * factor[4],
                factor[3] * factor[3] + factor[4] * factor[4] + factor[5] * factor[5],
            ]
            values[0] = weight
            for axis in range(3):
                values[1 + axis] = weight * centre[axis]
            for entry, (left, right) in enumerate(PAIRS):
                values[4 + entry] = weight * (spread[entry] + centre[left] * centre[right])
        for entry in range(colour_total):
            values[10 + first_colour + entry] = weight * colours[entry, part, :].astype(jnp.float32)
        for place, component in enumerate(components):
            moments[pl.ds(place * block_count + start, group), :] = values[component]
        return carry

    lax.fori_loop(0, block_count // group, prepare, 0)
    live = live_ref[0]

    def fold(step, carry):
        folded = []
        for turn in range(UNROLL):
            block = step * UNROLL + turn
            place = place_ref[block]
            region, slot = place // slots, place % slots
            lines = [
                moments[pl.ds(tile * TILE * block_count + block, TILE, stride=block_count), :]
                for tile in range(full)
            ]
            if extra:
                line = moments[pl.ds(full * TILE * block_count + block, TILE, stride=block_count), :]
                lines.append(jnp.where(tile_rows() // extra == slot % (TILE // extra), line, 0.0))
            rows = jnp.where(block < live, rows_ref[pl.ds(block, 1), :], -1)
            folded.append((region, slot, fold_block(jnp.concatenate(lines, 0), rows)))
        for region, slot, result in folded:
            for line, (at, tile) in enumerate(tiles):
                spot = starts[at] + region * sizes[at] + tile * slots + slot
                totals[spot] += result[line * TILE : (line + 1) * TILE]
            if extra:
                spot = starts[shared] + region * sizes[shared] + (widths[shared] // TILE) * slots
                totals[spot + slot // (TILE // extra)] += result[full * TILE :]
        return carry

    lax.fori_loop(0, (live + UNROLL - 1) // UNROLL, fold, 0)
    stores = []
    for at, size in enumerate(sizes):
        half = regions * size
        for turn in (1, 0):
            source = totals.at[pl.ds(starts[at] + turn * half, half)]
            store = pltpu.make_async_copy(source, out_refs[2 * at + turn], out_sems.at[2 * at + turn])
            store.start()
            stores.append(store)
    for store in stores:
        store.wait()


def fold_children(place, live, arrays, first, widths, regions, slots, vmem):
    rows, weight, mean, factor, colour = arrays
    colour_total = max(first + sum(widths) - max(first, 10), 0)
    used = [rows, weight] + ([mean, factor] if first == 0 else [])
    if colour_total:
        used.append(colour)
    block_count, row_count = rows.shape
    width = sum(widths)
    sizes = [tile_count(part, slots) for part in widths]
    padded = width // TILE * TILE + (TILE if width % TILE else 0)
    halves = [
        jax.ShapeDtypeStruct((regions * size, TILE, row_count), jnp.float32)
        for size in sizes
        for _ in range(2)
    ]
    scalars = pl.BlockSpec(memory_space=pltpu.SMEM)
    outside = pl.BlockSpec(memory_space=pl.ANY)
    targets = [pltpu.VMEM(array.shape, array.dtype) for array in used]
    if colour_total:
        targets[-1] = pltpu.VMEM((colour_total,) + colour.shape[1:], colour.dtype)

    def kernel(*refs):
        child_kernel(first, widths, regions, slots, *refs)

    return pl.pallas_call(
        kernel,
        out_shape=halves,
        in_specs=[scalars, scalars] + [outside] * len(used),
        out_specs=[outside] * len(halves),
        scratch_shapes=targets
        + [
            pltpu.VMEM((padded * block_count, row_count), jnp.float32),
            pltpu.VMEM((2 * regions * sum(sizes), TILE, row_count), jnp.float32),
            pltpu.SemaphoreType.DMA((len(used),)),
            pltpu.SemaphoreType.DMA((len(halves),)),
        ],
        compiler_params=pltpu.CompilerParams(vmem_limit_bytes=vmem * 1024 * 1024),
        cost_estimate=pl.CostEstimate(flops=1024, bytes_accessed=1024, transcendentals=0),
        name="fold_children",
    )(place, live, *used)


def group_sizes(widths, cap):
    full = sum(width // TILE for width in widths)
    extra = sum(width % TILE for width in widths)
    return full, extra, full * cap + (1 if extra else 0)


def parent_kernel(widths, owners, cap, coded, *refs):
    place_ref, code_ref, rows_ref = refs[:3]
    sums_refs = refs[3 : 3 + len(widths)]
    out_refs, totals = refs[3 + len(widths) : -1], refs[-1]
    block_count = rows_ref.shape[0]
    full, extra, used = group_sizes(widths, cap)
    per_owner = used + (1 if coded else 0)
    totals[...] = jnp.zeros(totals.shape, jnp.float32)
    for start in range(0, block_count, UNROLL):
        folded = []
        for block in range(start, start + UNROLL):
            place = place_ref[block]
            owner, rank = place // cap, place % cap
            lines, shared = [], []
            for width, sums_ref in zip(widths, sums_refs, strict=True):
                tiles = width // TILE
                lines += [sums_ref[tile * block_count + block] for tile in range(tiles)]
                if width % TILE:
                    share = TILE // extra
                    line = sums_ref[tiles * block_count + block // share]
                    line = spread_group(line, extra, block % share)
                    shared.append(jnp.where(tile_rows() // extra == rank, line, 0.0))
            rows = rows_ref[pl.ds(block, 1), :]
            result = fold_block(jnp.concatenate(lines + shared, 0), rows)
            folded.append((owner * per_owner, rank, result))
            if coded:
                code = code_ref[block].astype(jnp.float32)
                totals[owner * per_owner + used] += jnp.where(tile_rows() == rank, code, 0.0)
        for base, rank, result in folded:
            for tile in range(full):
                totals[base + tile * cap + rank] += result[tile * TILE : (tile + 1) * TILE]
            if extra:
                totals[base + full * cap] += result[full * TILE :]
    for owner, out_ref in enumerate(out_refs):
        out_ref[...] = totals[owner * per_owner : (owner + 1) * per_owner]


def fold_parents(place, code, rows, sums, widths, owners, cap, coded):
    row_count = rows.shape[1]
    per_owner = group_sizes(widths, cap)[2] + (1 if coded else 0)
    whole = pl.BlockSpec(memory_space=pltpu.VMEM)
    scalars = pl.BlockSpec(memory_space=pltpu.SMEM)

    def kernel(*refs):
        parent_kernel(widths, owners, cap, coded, *refs)

    return pl.pallas_call(
        kernel,
        out_shape=[jax.ShapeDtypeStruct((per_owner, TILE, row_count), jnp.float32)] * owners,
        in_specs=[scalars, scalars, whole] + [whole] * len(sums),
        out_specs=[whole] * owners,
        scratch_shapes=[pltpu.VMEM((owners * per_owner, TILE, row_count), jnp.float32)],
        compiler_params=pltpu.CompilerParams(vmem_limit_bytes=16 * 1024 * 1024),
        cost_estimate=pl.CostEstimate(flops=1024, bytes_accessed=1024, transcendentals=0),
        name="fold_parents",
    )(place, code, rows, *sums)


def place_kernel(widths, owners, cap, slots, coded, *refs):
    first_ref, in_refs, out_refs = refs[0], refs[1 : 1 + owners], refs[1 + owners :]
    keep_ref, send_ref = out_refs[:2]
    shape = in_refs[0].shape[1:]
    full, extra, used = group_sizes(widths, cap)
    if coded:
        for owner in range(owners):
            code = in_refs[owner][used].astype(jnp.int32)
            out_refs[2][owner] = (code // slots + first_ref[0]) % 2 * slots + code % slots
    codes_in = out_refs[2] if coded else first_ref
    for half, out_ref in enumerate((keep_ref, send_ref)):
        for slot in range(slots):
            label = half * slots + slot
            sums = [jnp.zeros(shape, jnp.float32) for _ in range(full)]
            for owner in range(owners):
                for rank in range(cap):
                    here = codes_in[owner, rank : rank + 1, :] == label
                    for tile in range(full):
                        line = in_refs[owner][tile * cap + rank]
                        sums[tile] += jnp.where(here, line, 0.0)
            for tile in range(full):
                out_ref[tile * slots + slot] = sums[tile]
        if extra:
            share = TILE // extra
            sums = [jnp.zeros(shape, jnp.float32) for _ in range(slots // share)]
            for owner in range(owners):
                for rank in range(cap):
                    line = spread_group(in_refs[owner][full * cap], extra, rank)
                    code = codes_in[owner, rank : rank + 1, :] - half * slots - tile_rows() // extra
                    for tile in range(slots // share):
                        sums[tile] += jnp.where(code == tile * share, line, 0.0)
            for tile in range(slots // share):
                out_ref[full * slots + tile] = sums[tile]


def place_parents(sub_at, codes, received, widths, owners, cap, slots):
    row_count = received[0].shape[2]
    coded = codes is None
    full, extra, _ = group_sizes(widths, cap)
    per_half = full * slots + slots * extra // TILE
    whole = pl.BlockSpec(memory_space=pltpu.VMEM)
    scalars = pl.BlockSpec(memory_space=pltpu.SMEM)
    half = jax.ShapeDtypeStruct((per_half, TILE, row_count), jnp.float32)
    table = jax.ShapeDtypeStruct((owners, TILE, row_count), jnp.int32)

    def kernel(*refs):
        place_kernel(widths, owners, cap, slots, coded, *refs)

    return pl.pallas_call(
        kernel,
        out_shape=(half, half, table) if coded else (half, half),
        in_specs=[scalars if coded else whole] + [whole] * owners,
        out_specs=(whole, whole, whole) if coded else (whole, whole),
        compiler_params=pltpu.CompilerParams(vmem_limit_bytes=16 * 1024 * 1024),
        cost_estimate=pl.CostEstimate(flops=1024, bytes_accessed=1024, transcendentals=0),
        name="place_parents",
    )(sub_at.reshape(1) if coded else codes, *received)


def unpack(tiles, widths, slots):
    row_count = tiles.shape[2]
    parts, start = [], 0
    for width in widths:
        full = width // TILE
        whole = tiles[start : start + full * slots].reshape(full, slots, TILE, row_count)
        parts.append([whole.transpose(0, 2, 1, 3).reshape(full * TILE, slots, row_count)])
        start += full * slots
    for part, width in zip(parts, widths, strict=True):
        if width % TILE:
            rest = tiles[start:].reshape(slots, width % TILE, row_count)
            part.append(rest.transpose(1, 0, 2))
    return [jnp.concatenate(part, 0) for part in parts]


def merged_parts(parts):
    sums = parts[0]
    divisor = jnp.maximum(sums[0], WEIGHT_FLOOR)
    centre = sums[1:4] / divisor
    centre_outer = jnp.stack([centre[first] * centre[second] for first, second in PAIRS])
    spread = sums[4:10] / divisor - centre_outer
    rest = [part / divisor for part in [sums[10:]] + parts[1:] if part.shape[0]]
    return jnp.concatenate([sums[:1], centre, spread] + rest, 0)


def cut_components(components):
    chunks, start = [(0, 10)], 10
    for width in WIDTHS:
        width = min(width, components - start)
        if width > 0:
            chunks.append((start, width))
            start += width
    if start < components:
        chunks.append((start, components - start))
    return chunks


def after(values, *others):
    return lax.optimization_barrier((values,) + others)[0]


def span_body(
    child_weight,
    child_mean,
    child_factor,
    child_colour,
    child_dest,
    child_slot,
    child_row,
    live_blocks,
    parent_owner,
    parent_slot,
    parent_row,
):
    spans = lax.axis_size("span")
    levels = spans.bit_length() - 1
    components = 10 + child_colour.shape[0]
    span_at, sub_at = lax.axis_index("span"), lax.axis_index("sub")
    cap_two = max(1, (PB_DEV + spans - 1) // spans)

    def swap(values):
        return lax.ppermute(values, "sub", [(0, 1), (1, 0)])

    def cross(values, bit):
        return lax.ppermute(values, "span", [(at, at ^ (1 << bit)) for at in range(spans)])

    away = child_dest ^ span_at
    half = (child_slot // PB_DEV + sub_at) % 2

    def place_in(order):
        region = sum(((away >> bit) & 1) << (levels - 1 - at) for at, bit in enumerate(order))
        return (half * spans + region) * PB_DEV + child_slot % PB_DEV

    place_two = (parent_owner ^ span_at) * cap_two + earlier_same(parent_owner)

    arrays = (child_row, child_weight, child_mean, child_factor, child_colour)
    chunks = cut_components(components)
    total = len(chunks)
    sizes = [tile_count(width, PB_DEV) for _, width in chunks]
    orders = [list(range(levels)) for _ in chunks]
    terms = [[] for _ in chunks]
    sends = [[] for _ in chunks]

    def fold(group, *others):
        place = place_in(orders[group[0]])
        if others:
            place = after(place, *others)
        widths = [chunks[at][1] for at in group]
        halves = fold_children(
            place, live_blocks, arrays, chunks[group[0]][0], widths, spans, PB_DEV, 56
        )
        for turn, at in enumerate(group):
            terms[at] = [halves[2 * turn], swap(halves[2 * turn + 1])]

    def part(at, low, high):
        return sum(
            (term[low * sizes[at] : high * sizes[at]] for term in terms[at][1:]),
            start=terms[at][0][low * sizes[at] : high * sizes[at]],
        )

    def exchange(at, level, *others):
        low = spans >> (level + 1)
        send = part(at, low, 2 * low)
        if others:
            send = after(send, *others)
        sends[at].append(send)
        terms[at].append(cross(send, orders[at][level]))

    def send_of(at, level):
        low = spans >> (level + 1)
        return part(at, low, 2 * low)

    def depart(at, level, send):
        terms[at].append(cross(send, orders[at][level]))

    def depart_alone(at, level):
        send = send_of(at, level)
        depart(at, level, send)
        return send

    level_one, level_two, codes, fetched = [], [], [None], []

    def unpack_one():
        return [
            unpack(sums[at], [width], PB_DEV)[0] for at, (_, width) in enumerate(chunks)
        ]


    def raise_level(group, *others):
        widths = [chunks[at][1] for at in group]
        parts = fold_parents(
            after(place_two, *others) if others else place_two,
            parent_slot,
            parent_row,
            [sums[at] for at in group],
            widths,
            spans,
            cap_two,
            codes[0] is None,
        )
        parts = [
            lax.ppermute(part, "span", [(at, at ^ away) for at in range(spans)]) if away else part
            for away, part in enumerate(parts)
        ]
        fetched.append(parts[-1])
        level_one.append(merged_parts(unpack_one()))
        parts = [after(part, level_one[0]) for part in parts]
        placed = place_parents(sub_at, codes[0], parts, widths, spans, cap_two, GB_DEV)
        if codes[0] is None:
            codes[0] = placed[2]
        level_two.extend(unpack(placed[0] + swap(placed[1]), widths, GB_DEV))

    fold(list(range(total)))
    depart_alone(0, 0)
    depart_alone(1, 0)
    sums = [None] * total
    last, size = total - 1, sizes[total - 1]
    lines = []

    def here(*regions):
        return jnp.concatenate([part(last, region, region + 1) for region in regions], 0)

    def line_send(step):
        if step == 0:
            return here(2, 3, 6, 7)
        if step == 1:
            return here(1, 5) + jnp.concatenate([lines[0][size : 2 * size], lines[0][3 * size :]], 0)
        return here(4) + lines[0][2 * size : 3 * size] + lines[1][size:]

    def line_depart(step, send):
        lines.append(cross(send, (1, 2, 0)[step]))
        if step == 2:
            sums[last] = here(0) + lines[0][:size] + lines[1][:size] + lines[2]

    line_depart(0, line_send(0))
    for phase in range(last + levels - 2):
        moves, done = [], []
        if phase + 2 < last:
            moves.append((phase + 2, 0))
        for turn in range(levels - 1):
            if 0 <= phase - turn < last:
                moves.append((phase - turn, turn + 1))
        if phase >= levels - 1:
            done.append(terms[phase - levels + 1][-1])
        ready = [send_of(at, level) for at, level in moves]
        if phase in LINE_FIRST:
            moves.append((last, LINE_FIRST[phase]))
            ready.append(line_send(LINE_FIRST[phase]))
        ready = lax.optimization_barrier(tuple(ready + done))[: len(ready)]
        for (at, level), send in zip(moves, ready, strict=True):
            if at == last:
                line_depart(level, send)
                continue
            depart(at, level, send)
            if level == levels - 1:
                sums[at] = part(at, 0, 1)
    raise_level(list(range(total)))
    return (level_one[0], merged_parts(level_two))


def body(*arrays):
    spans, subs = lax.axis_size("span"), lax.axis_size("sub")
    blocks = arrays[0].shape[0]
    dense = spans * subs * PB_DEV
    fits = subs == 2 and spans & (spans - 1) == 0 and dense <= 4 * blocks
    if fits and PB_DEV == 4 * spans and blocks % 16 == 0:
        return span_body(*arrays)
    return plain_body(*arrays)


def solution(mesh):
    placed = (
        P(("groups", "span", "sub"), None),
        P(None, ("groups", "span", "sub"), None),
        P(None, ("groups", "span", "sub"), None),
        P(None, ("groups", "span", "sub"), None),
        P(("groups", "span", "sub")),
        P(("groups", "span", "sub")),
        P(("groups", "span", "sub"), None),
        P(("groups", "span", "sub")),
        P(("groups", "span", "sub")),
        P(("groups", "span", "sub")),
        P(("groups", "span", "sub"), None),
    )
    return jax.shard_map(
        body,
        mesh=mesh,
        in_specs=placed,
        out_specs=(
            P(None, ("groups", "span", "sub"), None),
            P(None, ("groups", "span", "sub"), None),
        ),
        check_vma=False,
    )
```

```python
import math

import jax
import jax.numpy as jnp
from jax import lax
from jax.experimental import pallas as pl
from jax.experimental.pallas import tpu as pltpu
from jax.sharding import PartitionSpec as P

PB_DEV = 32
GB_DEV = 8


PAIRS = ((0, 0), (0, 1), (0, 2), (1, 1), (1, 2), (2, 2))
WEIGHT_FLOOR = 0.1


def covariance(factor):
    return jnp.stack(
        [
            factor[0] * factor[0],
            factor[0] * factor[1],
            factor[0] * factor[3],
            factor[1] * factor[1] + factor[2] * factor[2],
            factor[1] * factor[3] + factor[2] * factor[4],
            factor[3] * factor[3] + factor[4] * factor[4] + factor[5] * factor[5],
        ]
    )


def moment_sums(weight, centres, factor, colour):
    outer = jnp.stack([centres[first] * centres[second] for first, second in PAIRS])
    return jnp.concatenate(
        [
            weight[None],
            weight * centres,
            weight * (covariance(factor) + outer),
            weight * colour.astype(jnp.float32),
        ],
        0,
    )


def match_moments(sums):
    whole_weight = sums[0]
    divisor = jnp.maximum(whole_weight, WEIGHT_FLOOR)
    centre = sums[1:4] / divisor
    centre_outer = jnp.stack([centre[first] * centre[second] for first, second in PAIRS])
    spread = sums[4:10] / divisor - centre_outer
    colour_mean = sums[10:] / divisor
    return jnp.concatenate([whole_weight[None], centre, spread, colour_mean], 0)


def earlier_same(owners):
    position = jnp.arange(owners.shape[0], dtype=jnp.int32)
    same_owner = (owners[:, None] == owners[None, :]) & (position[None, :] < position[:, None])
    return jnp.sum(same_owner.astype(jnp.int32), 1)


def fold_rows(values, row_picks):
    block_total = values.shape[1]
    width = values.shape[2]
    group_size = math.gcd(block_total, 16)
    row_labels = jnp.arange(width, dtype=jnp.int32)

    def fold_step(turn_index, result):
        start = turn_index * group_size
        block_part = lax.dynamic_slice_in_dim(values, start, group_size, 1)
        picks_part = lax.dynamic_slice_in_dim(row_picks, start, group_size, 0)
        row_table = (picks_part[:, :, None] == row_labels).astype(jnp.float32)
        folded_part = jnp.einsum(
            "cbr,brj->cbj", block_part, row_table, precision=lax.Precision.HIGHEST
        )
        return lax.dynamic_update_slice_in_dim(result, folded_part, start, 1)

    return lax.fori_loop(
        0, block_total // group_size, fold_step, jnp.zeros(values.shape, jnp.float32)
    )


def place_blocks(values, block_picks, block_count):
    block_table = (block_picks[:, None] == jnp.arange(block_count, dtype=jnp.int32)).astype(
        jnp.float32
    )
    return jnp.einsum("csj,sp->cpj", values, block_table, precision=lax.Precision.HIGHEST)


def seam(partial_value, per_device):
    whole_sum = lax.psum(partial_value, "sub")
    return lax.dynamic_slice_in_dim(whole_sum, lax.axis_index("sub") * per_device, per_device, 1)


def plain_body(
    child_weight,
    child_mean,
    child_factor,
    child_colour,
    child_dest,
    child_slot,
    child_row,
    live_blocks,
    parent_owner,
    parent_slot,
    parent_row,
):
    spans = lax.axis_size("span")
    sub_count = lax.axis_size("sub")
    block_count = child_weight.shape[0]
    row_count = child_weight.shape[1]
    components = 10 + child_colour.shape[0]
    cap_one = max(2, (2 * block_count + spans - 1) // spans)
    slot_total = spans * cap_one
    parent_span = PB_DEV * sub_count
    moments = moment_sums(child_weight, child_mean, child_factor, child_colour)
    position = jnp.arange(block_count, dtype=jnp.int32)
    is_live = position < live_blocks[0]
    slot_index = jnp.where(is_live, child_dest * cap_one + earlier_same(child_dest), slot_total)
    outgoing_shape = (components, slot_total, row_count)
    outgoing = jnp.zeros(outgoing_shape, jnp.float32).at[:, slot_index].set(moments, mode="drop")
    targets = child_slot[:, None] * row_count + child_row
    target_rows = (
        jnp.zeros((1, slot_total, row_count), jnp.int32).at[0, slot_index].set(targets, mode="drop")
    )
    received, received_rows = (
        lax.all_to_all(outgoing, "span", split_axis=1, concat_axis=1, tiled=True),
        lax.all_to_all(target_rows, "span", split_axis=1, concat_axis=1, tiled=True),
    )
    incoming_rows = received_rows[0]
    folded = fold_rows(received, incoming_rows % row_count)
    collected = place_blocks(folded, incoming_rows[:, 0] // row_count, parent_span)
    own_sums = seam(collected, PB_DEV)
    level_one = match_moments(own_sums)
    cap_two = max(1, (PB_DEV + spans - 1) // spans)
    slot_two = parent_owner * cap_two + earlier_same(parent_owner)
    outgoing_two = (
        jnp.zeros((components, spans * cap_two, row_count), jnp.float32)
        .at[:, slot_two]
        .set(own_sums)
    )
    targets_two = parent_slot[:, None] * row_count + parent_row
    rows_two = (
        jnp.zeros((1, spans * cap_two, row_count), jnp.int32).at[0, slot_two].set(targets_two)
    )
    received_two, received_rows_two = (
        lax.all_to_all(outgoing_two, "span", split_axis=1, concat_axis=1, tiled=True),
        lax.all_to_all(rows_two, "span", split_axis=1, concat_axis=1, tiled=True),
    )
    grand_span = GB_DEV * sub_count
    incoming_two = received_rows_two[0]
    folded_two = fold_rows(received_two, incoming_two % row_count)
    collected_two = place_blocks(folded_two, incoming_two[:, 0] // row_count, grand_span)
    level_two = match_moments(seam(collected_two, GB_DEV))
    return (level_one, level_two)


TILE = 8
UNROLL = 8
LINE_FIRST = {0: 1, 3: 2}


def tile_count(width, slots):
    return (width // TILE) * slots + (slots * (width % TILE) + TILE - 1) // TILE


def split_pair(values):
    high = values.astype(jnp.bfloat16)
    low = (values - high.astype(jnp.float32)).astype(jnp.bfloat16)
    return jnp.concatenate([high, low], 1)


def row_table(rows):
    width = rows.shape[1]
    labels = lax.broadcasted_iota(jnp.int32, (width, width), 0)
    picks = jnp.where(labels == rows, 1.0, 0.0).astype(jnp.bfloat16)
    return jnp.concatenate([picks, picks], 1)


def fold_block(values, rows):
    return lax.dot_general(
        split_pair(values),
        row_table(rows),
        (((1,), (1,)), ((), ())),
        preferred_element_type=jnp.float32,
    )


def tile_rows():
    return lax.broadcasted_iota(jnp.int32, (TILE, 1), 0)


def spread_group(line, extra, group):
    share = TILE // extra
    line = jnp.where(tile_rows() // extra == group, line, 0.0)
    return sum((pltpu.roll(line, turn * extra, 0) for turn in range(1, share)), start=line)


def child_kernel(first, widths, regions, slots, *refs):
    geometry = first == 0
    colour_total = max(first + sum(widths) - max(first, 10), 0)
    place_ref, live_ref = refs[:2]
    count = 2 + 2 * geometry + (colour_total > 0)
    sources = refs[2 : 2 + count]
    refs = refs[2 + count :]
    out_refs, refs = refs[: 2 * len(widths)], refs[2 * len(widths) :]
    targets = refs[:count]
    rows_ref, weight_ref = targets[:2]
    moments, totals, load_sems, out_sems = refs[count:]
    block_count, row_count = rows_ref.shape
    width = sum(widths)
    sizes = [tile_count(part, slots) for part in widths]
    starts = [2 * regions * sum(sizes[:at]) for at in range(len(sizes))]
    tiles = [(at, tile) for at, part in enumerate(widths) for tile in range(part // TILE)]
    bases = [first + sum(widths[:at]) for at in range(len(widths))]
    components = [bases[at] + tile * TILE + line for at, tile in tiles for line in range(TILE)]
    full, extra = len(tiles), 0
    for at, part in enumerate(widths):
        if part % TILE:
            extra, shared = part % TILE, at
            components += [bases[at] + part - extra + line % extra for line in range(TILE)]
    group = 16
    first_colour = max(first, 10) - 10
    loads = []
    for at, (source, target) in enumerate(zip(sources, targets, strict=True)):
        if colour_total and at == count - 1:
            source = source.at[pl.ds(first_colour, colour_total)]
        loads.append(pltpu.make_async_copy(source, target, load_sems.at[at]))
    if geometry:
        mean_ref, factor_ref = targets[2:4]
    colours = targets[-1]
    for load in loads:
        load.start()

    def clear(step, carry):
        totals[pl.ds(step * 16, 16)] = jnp.zeros((16, TILE, row_count), jnp.float32)
        return carry

    lax.fori_loop(0, totals.shape[0] // 16, clear, 0)
    for load in loads:
        load.wait()

    def prepare(step, carry):
        start = pl.multiple_of(step * group, group)
        part = pl.ds(start, group)
        weight = weight_ref[part, :]
        values = {}
        if geometry:
            centre = [mean_ref[axis, part, :] for axis in range(3)]
            factor = [factor_ref[entry, part, :] for entry in range(6)]
            spread = [
                factor[0] * factor[0],
                factor[0] * factor[1],
                factor[0] * factor[3],
                factor[1] * factor[1] + factor[2] * factor[2],
                factor[1] * factor[3] + factor[2] * factor[4],
                factor[3] * factor[3] + factor[4] * factor[4] + factor[5] * factor[5],
            ]
            values[0] = weight
            for axis in range(3):
                values[1 + axis] = weight * centre[axis]
            for entry, (left, right) in enumerate(PAIRS):
                values[4 + entry] = weight * (spread[entry] + centre[left] * centre[right])
        for entry in range(colour_total):
            values[10 + first_colour + entry] = weight * colours[entry, part, :].astype(jnp.float32)
        for place, component in enumerate(components):
            moments[pl.ds(place * block_count + start, group), :] = values[component]
        return carry

    lax.fori_loop(0, block_count // group, prepare, 0)
    live = live_ref[0]

    def fold(step, carry):
        folded = []
        for turn in range(UNROLL):
            block = step * UNROLL + turn
            place = place_ref[block]
            region, slot = place // slots, place % slots
            lines = [
                moments[pl.ds(tile * TILE * block_count + block, TILE, stride=block_count), :]
                for tile in range(full)
            ]
            if extra:
                line = moments[pl.ds(full * TILE * block_count + block, TILE, stride=block_count), :]
                lines.append(jnp.where(tile_rows() // extra == slot % (TILE // extra), line, 0.0))
            rows = jnp.where(block < live, rows_ref[pl.ds(block, 1), :], -1)
            folded.append((region, slot, fold_block(jnp.concatenate(lines, 0), rows)))
        for region, slot, result in folded:
            for line, (at, tile) in enumerate(tiles):
                spot = starts[at] + region * sizes[at] + tile * slots + slot
                totals[spot] += result[line * TILE : (line + 1) * TILE]
            if extra:
                spot = starts[shared] + region * sizes[shared] + (widths[shared] // TILE) * slots
                totals[spot + slot // (TILE // extra)] += result[full * TILE :]
        return carry

    lax.fori_loop(0, (live + UNROLL - 1) // UNROLL, fold, 0)
    stores = []
    for at, size in enumerate(sizes):
        half = regions * size
        for turn in (1, 0):
            source = totals.at[pl.ds(starts[at] + turn * half, half)]
            store = pltpu.make_async_copy(source, out_refs[2 * at + turn], out_sems.at[2 * at + turn])
            store.start()
            stores.append(store)
    for store in stores:
        store.wait()


def fold_children(place, live, arrays, first, widths, regions, slots, vmem):
    rows, weight, mean, factor, colour = arrays
    colour_total = max(first + sum(widths) - max(first, 10), 0)
    used = [rows, weight] + ([mean, factor] if first == 0 else [])
    if colour_total:
        used.append(colour)
    block_count, row_count = rows.shape
    width = sum(widths)
    sizes = [tile_count(part, slots) for part in widths]
    padded = width // TILE * TILE + (TILE if width % TILE else 0)
    halves = [
        jax.ShapeDtypeStruct((regions * size, TILE, row_count), jnp.float32)
        for size in sizes
        for _ in range(2)
    ]
    scalars = pl.BlockSpec(memory_space=pltpu.SMEM)
    outside = pl.BlockSpec(memory_space=pl.ANY)
    targets = [pltpu.VMEM(array.shape, array.dtype) for array in used]
    if colour_total:
        targets[-1] = pltpu.VMEM((colour_total,) + colour.shape[1:], colour.dtype)

    def kernel(*refs):
        child_kernel(first, widths, regions, slots, *refs)

    return pl.pallas_call(
        kernel,
        out_shape=halves,
        in_specs=[scalars, scalars] + [outside] * len(used),
        out_specs=[outside] * len(halves),
        scratch_shapes=targets
        + [
            pltpu.VMEM(((padded + 1) * block_count, row_count), jnp.float32),
            pltpu.VMEM((2 * regions * sum(sizes), TILE, row_count), jnp.float32),
            pltpu.SemaphoreType.DMA((len(used),)),
            pltpu.SemaphoreType.DMA((len(halves),)),
        ],
        compiler_params=pltpu.CompilerParams(vmem_limit_bytes=vmem * 1024 * 1024),
        cost_estimate=pl.CostEstimate(flops=1024, bytes_accessed=1024, transcendentals=0),
        name="fold_children",
    )(place, live, *used)


def group_sizes(widths, cap):
    full = sum(width // TILE for width in widths)
    extra = sum(width % TILE for width in widths)
    return full, extra, full * cap + (1 if extra else 0)


def parent_kernel(widths, owners, cap, coded, *refs):
    place_ref, code_ref, rows_ref = refs[:3]
    sums_refs = refs[3 : 3 + len(widths)]
    out_refs, totals = refs[3 + len(widths) : -1], refs[-1]
    block_count = rows_ref.shape[0]
    full, extra, used = group_sizes(widths, cap)
    per_owner = used + (1 if coded else 0)
    totals[...] = jnp.zeros(totals.shape, jnp.float32)
    for start in range(0, block_count, UNROLL):
        folded = []
        for block in range(start, start + UNROLL):
            place = place_ref[block]
            owner, rank = place // cap, place % cap
            lines, shared = [], []
            for width, sums_ref in zip(widths, sums_refs, strict=True):
                tiles = width // TILE
                lines += [sums_ref[tile * block_count + block] for tile in range(tiles)]
                if width % TILE:
                    share = TILE // extra
                    line = sums_ref[tiles * block_count + block // share]
                    line = spread_group(line, extra, block % share)
                    shared.append(jnp.where(tile_rows() // extra == rank, line, 0.0))
            rows = rows_ref[pl.ds(block, 1), :]
            result = fold_block(jnp.concatenate(lines + shared, 0), rows)
            folded.append((owner * per_owner, rank, result))
            if coded:
                code = code_ref[block].astype(jnp.float32)
                totals[owner * per_owner + used] += jnp.where(tile_rows() == rank, code, 0.0)
        for base, rank, result in folded:
            for tile in range(full):
                totals[base + tile * cap + rank] += result[tile * TILE : (tile + 1) * TILE]
            if extra:
                totals[base + full * cap] += result[full * TILE :]
    for owner, out_ref in enumerate(out_refs):
        out_ref[...] = totals[owner * per_owner : (owner + 1) * per_owner]


def fold_parents(place, code, rows, sums, widths, owners, cap, coded):
    row_count = rows.shape[1]
    per_owner = group_sizes(widths, cap)[2] + (1 if coded else 0)
    whole = pl.BlockSpec(memory_space=pltpu.VMEM)
    scalars = pl.BlockSpec(memory_space=pltpu.SMEM)

    def kernel(*refs):
        parent_kernel(widths, owners, cap, coded, *refs)

    return pl.pallas_call(
        kernel,
        out_shape=[jax.ShapeDtypeStruct((per_owner, TILE, row_count), jnp.float32)] * owners,
        in_specs=[scalars, scalars, whole] + [whole] * len(sums),
        out_specs=[whole] * owners,
        scratch_shapes=[pltpu.VMEM((owners * per_owner, TILE, row_count), jnp.float32)],
        compiler_params=pltpu.CompilerParams(vmem_limit_bytes=16 * 1024 * 1024),
        cost_estimate=pl.CostEstimate(flops=1024, bytes_accessed=1024, transcendentals=0),
        name="fold_parents",
    )(place, code, rows, *sums)


def place_kernel(widths, owners, cap, slots, coded, *refs):
    first_ref, in_refs, out_refs = refs[0], refs[1 : 1 + owners], refs[1 + owners :]
    keep_ref, send_ref = out_refs[:2]
    shape = in_refs[0].shape[1:]
    full, extra, used = group_sizes(widths, cap)
    if coded:
        for owner in range(owners):
            code = in_refs[owner][used].astype(jnp.int32)
            out_refs[2][owner] = (code // slots + first_ref[0]) % 2 * slots + code % slots
    codes_in = out_refs[2] if coded else first_ref
    for half, out_ref in enumerate((keep_ref, send_ref)):
        for slot in range(slots):
            label = half * slots + slot
            sums = [jnp.zeros(shape, jnp.float32) for _ in range(full)]
            for owner in range(owners):
                for rank in range(cap):
                    here = codes_in[owner, rank : rank + 1, :] == label
                    for tile in range(full):
                        line = in_refs[owner][tile * cap + rank]
                        sums[tile] += jnp.where(here, line, 0.0)
            for tile in range(full):
                out_ref[tile * slots + slot] = sums[tile]
        if extra:
            share = TILE // extra
            sums = [jnp.zeros(shape, jnp.float32) for _ in range(slots // share)]
            for owner in range(owners):
                for rank in range(cap):
                    line = spread_group(in_refs[owner][full * cap], extra, rank)
                    code = codes_in[owner, rank : rank + 1, :] - half * slots - tile_rows() // extra
                    for tile in range(slots // share):
                        sums[tile] += jnp.where(code == tile * share, line, 0.0)
            for tile in range(slots // share):
                out_ref[full * slots + tile] = sums[tile]


def place_parents(sub_at, codes, received, widths, owners, cap, slots):
    row_count = received[0].shape[2]
    coded = codes is None
    full, extra, _ = group_sizes(widths, cap)
    per_half = full * slots + slots * extra // TILE
    whole = pl.BlockSpec(memory_space=pltpu.VMEM)
    scalars = pl.BlockSpec(memory_space=pltpu.SMEM)
    half = jax.ShapeDtypeStruct((per_half, TILE, row_count), jnp.float32)
    table = jax.ShapeDtypeStruct((owners, TILE, row_count), jnp.int32)

    def kernel(*refs):
        place_kernel(widths, owners, cap, slots, coded, *refs)

    return pl.pallas_call(
        kernel,
        out_shape=(half, half, table) if coded else (half, half),
        in_specs=[scalars if coded else whole] + [whole] * owners,
        out_specs=(whole, whole, whole) if coded else (whole, whole),
        compiler_params=pltpu.CompilerParams(vmem_limit_bytes=16 * 1024 * 1024),
        cost_estimate=pl.CostEstimate(flops=1024, bytes_accessed=1024, transcendentals=0),
        name="place_parents",
    )(sub_at.reshape(1) if coded else codes, *received)


def unpack(tiles, width, slots):
    full, extra = width // TILE, width % TILE
    row_count = tiles.shape[2]
    whole = tiles[: full * slots].reshape(full, slots, TILE, row_count)
    whole = whole.transpose(0, 2, 1, 3).reshape(full * TILE, slots, row_count)
    if not extra:
        return whole
    rest = tiles[full * slots :].reshape(slots, extra, row_count).transpose(1, 0, 2)
    return jnp.concatenate([whole, rest], 0)


def merged_parts(parts):
    sums = parts[0]
    divisor = jnp.maximum(sums[0], WEIGHT_FLOOR)
    centre = sums[1:4] / divisor
    centre_outer = jnp.stack([centre[first] * centre[second] for first, second in PAIRS])
    spread = sums[4:10] / divisor - centre_outer
    rest = [part / divisor for part in parts[1:]]
    return jnp.concatenate([sums[:1], centre, spread] + rest, 0)


def merge_kernel(colours, slots, tile, extra, out_ref):
    rows = tile_rows()
    for slot in range(slots):
        sums = tile(0, slot)
        scale = 1.0 / jnp.maximum(sums[:1], WEIGHT_FLOOR)
        means = sums * scale
        east, north, up = means[1:2], means[2:3], means[3:4]
        left = jnp.where(rows == 7, north, east)
        right = jnp.where(rows == 4, east, jnp.where(rows == 6, up, north))
        means = jnp.where(rows >= 4, means - left * right, means)
        out_ref[pl.ds(slot, TILE, stride=slots), :] = jnp.where(rows == 0, sums, means)
        share = 2 * (slot % (TILE // 2))
        rest = extra(slot // (TILE // 2))[share : share + 2] * scale
        out_ref[pl.ds(TILE * slots + slot, 1), :] = rest[:1] - north * up
        out_ref[pl.ds((TILE + 1) * slots + slot, 1), :] = rest[1:] - up * up
        for line in range(colours):
            start = (10 + line * TILE) * slots + slot
            out_ref[pl.ds(start, TILE, stride=slots), :] = tile(1 + line, slot) * scale


def merge_sums(sums, colours, slots, together):
    row_count = sums[0].shape[2]
    components = 10 + colours * TILE

    def kernel(*refs):
        ins, out_ref = refs[:-1], refs[-1]

        def tile(line, slot):
            if together:
                return ins[0][line * slots + slot] + ins[1][line * slots + slot]
            return ins[line][slot]

        def extra(at):
            if together:
                place = (1 + colours) * slots + at
                return ins[0][place] + ins[1][place]
            return ins[0][slots + at]

        merge_kernel(colours, slots, tile, extra, out_ref)

    whole = pl.BlockSpec(memory_space=pltpu.VMEM)
    merged = pl.pallas_call(
        kernel,
        out_shape=jax.ShapeDtypeStruct((components * slots, row_count), jnp.float32),
        in_specs=[whole] * len(sums),
        out_specs=whole,
        compiler_params=pltpu.CompilerParams(vmem_limit_bytes=16 * 1024 * 1024),
        cost_estimate=pl.CostEstimate(flops=1024, bytes_accessed=1024, transcendentals=0),
        name="merge_sums",
    )(*sums)
    return merged.reshape(components, slots, row_count)


def cut_components(components):
    return [(0, 10)] + [(start, TILE) for start in range(10, components, TILE)]


def after(values, *others):
    return lax.optimization_barrier((values,) + others)[0]


def span_body(
    child_weight,
    child_mean,
    child_factor,
    child_colour,
    child_dest,
    child_slot,
    child_row,
    live_blocks,
    parent_owner,
    parent_slot,
    parent_row,
):
    spans = lax.axis_size("span")
    levels = spans.bit_length() - 1
    components = 10 + child_colour.shape[0]
    span_at, sub_at = lax.axis_index("span"), lax.axis_index("sub")
    cap_two = max(1, (PB_DEV + spans - 1) // spans)

    def swap(values):
        return lax.ppermute(values, "sub", [(0, 1), (1, 0)])

    def cross(values, bit):
        return lax.ppermute(values, "span", [(at, at ^ (1 << bit)) for at in range(spans)])

    away = child_dest ^ span_at
    half = (child_slot // PB_DEV + sub_at) % 2

    def place_in(order):
        region = sum(((away >> bit) & 1) << (levels - 1 - at) for at, bit in enumerate(order))
        return (half * spans + region) * PB_DEV + child_slot % PB_DEV

    place_two = (parent_owner ^ span_at) * cap_two + earlier_same(parent_owner)

    arrays = (child_row, child_weight, child_mean, child_factor, child_colour)
    chunks = cut_components(components)
    total = len(chunks)
    sizes = [tile_count(width, PB_DEV) for _, width in chunks]
    orders = [list(range(levels)) for _ in chunks]
    terms = [[] for _ in chunks]

    def fold(group, *others):
        place = place_in(orders[group[0]])
        if others:
            place = after(place, *others)
        widths = [chunks[at][1] for at in group]
        halves = fold_children(
            place, live_blocks, arrays, chunks[group[0]][0], widths, spans, PB_DEV, 56
        )
        for turn, at in enumerate(group):
            terms[at] = [halves[2 * turn], swap(halves[2 * turn + 1])]

    def part(at, low, high):
        return sum(
            (term[low * sizes[at] : high * sizes[at]] for term in terms[at][1:]),
            start=terms[at][0][low * sizes[at] : high * sizes[at]],
        )

    def exchange(at, level, *others):
        low = spans >> (level + 1)
        send = part(at, low, 2 * low)
        if others:
            send = after(send, *others)
        sends[at].append(send)
        terms[at].append(cross(send, orders[at][level]))

    def send_of(at, level):
        low = spans >> (level + 1)
        return part(at, low, 2 * low)

    def depart(at, level, send):
        terms[at].append(cross(send, orders[at][level]))

    def depart_alone(at, level):
        send = send_of(at, level)
        depart(at, level, send)
        return send

    level_one, level_two, codes = [], [], [None]
    colours = total - 1

    def raise_level(group, *others):
        widths = [chunks[at][1] for at in group]
        parts = fold_parents(
            after(place_two, *others) if others else place_two,
            parent_slot,
            parent_row,
            [sums[at] for at in group],
            widths,
            spans,
            cap_two,
            codes[0] is None,
        )
        parts = [
            lax.ppermute(part, "span", [(at, at ^ away) for at in range(spans)]) if away else part
            for away, part in enumerate(parts)
        ]
        parted = zip(sums, chunks, strict=True)
        level_one.append(merged_parts([unpack(part, width, PB_DEV) for part, (_, width) in parted]))
        parts = [after(part, level_one[0]) for part in parts]
        placed = place_parents(sub_at, codes[0], parts, widths, spans, cap_two, GB_DEV)
        if codes[0] is None:
            codes[0] = placed[2]
        level_two.append(merge_sums([placed[0], swap(placed[1])], colours, GB_DEV, True))

    fold(list(range(total)))
    depart_alone(0, 0)
    depart_alone(1, 0)
    sums = [None] * total
    last, size = total - 1, sizes[total - 1]
    lines = []

    def here(*regions):
        return jnp.concatenate([part(last, region, region + 1) for region in regions], 0)

    def line_send(step):
        if step == 0:
            return here(2, 3, 6, 7)
        if step == 1:
            return here(1, 5) + jnp.concatenate([lines[0][size : 2 * size], lines[0][3 * size :]], 0)
        return here(4) + lines[0][2 * size : 3 * size] + lines[1][size:]

    def line_depart(step, send):
        lines.append(cross(send, (1, 2, 0)[step]))
        if step == 2:
            sums[last] = here(0) + lines[0][:size] + lines[1][:size] + lines[2]

    line_depart(0, line_send(0))
    for phase in range(last + levels - 2):
        moves, done = [], []
        if phase + 2 < last:
            moves.append((phase + 2, 0))
        for turn in range(levels - 1):
            if 0 <= phase - turn < last:
                moves.append((phase - turn, turn + 1))
        if phase >= levels - 1:
            done.append(terms[phase - levels + 1][-1])
        ready = [send_of(at, level) for at, level in moves]
        if phase in LINE_FIRST:
            moves.append((last, LINE_FIRST[phase]))
            ready.append(line_send(LINE_FIRST[phase]))
        ready = lax.optimization_barrier(tuple(ready + done))[: len(ready)]
        for (at, level), send in zip(moves, ready, strict=True):
            if at == last:
                line_depart(level, send)
                continue
            depart(at, level, send)
            if level == levels - 1:
                sums[at] = part(at, 0, 1)
    raise_level(list(range(total)))
    return (level_one[0], level_two[0])


def body(*arrays):
    spans, subs = lax.axis_size("span"), lax.axis_size("sub")
    blocks = arrays[0].shape[0]
    dense = spans * subs * PB_DEV
    fits = subs == 2 and spans & (spans - 1) == 0 and dense <= 4 * blocks
    colours = arrays[3].shape[0]
    if fits and PB_DEV == 4 * spans and blocks % 16 == 0 and colours % TILE == 0:
        return span_body(*arrays)
    return plain_body(*arrays)


def solution(mesh):
    placed = (
        P(("groups", "span", "sub"), None),
        P(None, ("groups", "span", "sub"), None),
        P(None, ("groups", "span", "sub"), None),
        P(None, ("groups", "span", "sub"), None),
        P(("groups", "span", "sub")),
        P(("groups", "span", "sub")),
        P(("groups", "span", "sub"), None),
        P(("groups", "span", "sub")),
        P(("groups", "span", "sub")),
        P(("groups", "span", "sub")),
        P(("groups", "span", "sub"), None),
    )
    return jax.shard_map(
        body,
        mesh=mesh,
        in_specs=placed,
        out_specs=(
            P(None, ("groups", "span", "sub"), None),
            P(None, ("groups", "span", "sub"), None),
        ),
        check_vma=False,
    )
```
